32 devices in a mesh: groups: 2 (over x), attn: 16 (over z, y, core).
Axes of the slice: x: 2, y: 2, z: 4, core: 2. Of those that a mesh axis runs over, the one named last changes fastest.
Arguments:
- queries: bfloat16 [256, 6144], P(('groups', 'attn')), parts along dimension 0, may hold values from -6 to 6
- kv_cache: bfloat16 [256, 48, 2048], P(('groups', 'attn')), parts along dimension 0, may hold values from -6 to 6
- lengths: int32 [256], P(('groups', 'attn')), parts along dimension 0, may hold values from 2 to 48, as said below
- handoff: int32 [32, 2], P(('groups', 'attn')), parts along dimension 0, may hold values from 0 to 7, as said below
- routes: int32 [256, 1], P(('groups', 'attn')), parts along dimension 0, may hold values from 0 to 1; in each aligned block of 8 rows (0 to 7, 8 to 15, ...) at most 6 rows name the same one
- norm_gain: bfloat16 [6144], replicated, may hold values from 0.099609375 to 1.8984375
- router: bfloat16 [6144, 2], replicated, may hold values from -0.078125 to 0.078125
- gate_proj: bfloat16 [6144, 16384], P(None, 'attn'), may hold values from -0.078125 to 0.078125
- up_proj: bfloat16 [6144, 16384], P(None, 'attn'), may hold values from -0.078125 to 0.078125
- down_proj: bfloat16 [16384, 6144], P('attn'), may hold values from -0.0625 to 0.0625
Outputs:
- mixed: bfloat16 [256, 6144], P(('groups', 'attn')), parts along dimension 0
The draws below stay inside these ranges and needn't reach their ends.
There are 2 independent parts, one for each index of `groups`. The reference program is written for one: setup_inputs(seed, part) draws one part's arguments, and reference() takes and returns one part's arrays. A program takes and returns all parts, laid end to end along the dimension named above; an argument that names none is the same for every part. Nothing has to cross between parts.
Inputs may be any that keep to these rules, and one draw needn't show every extreme that they name: `lengths`: some request has 48 cached positions. `handoff`: each row names 2 different local slots; the requests in them go to the device whose index differs in the highest bit. `routes`: in each aligned block of 8 rows (the slots of one device) no expert is named by more than 6 rows.
All inputs are finite; a program needn't handle non-finite values.
Results may differ from the reference program's by a relative error of at most 0.014.
Values may be sent and summed in bfloat16 or wider, within the bound.
A program may use at most 128 MiB of HBM per device.

```python
import math
import jax
import jax.numpy as jnp
import numpy as np
from jax import lax

D = 6144
HQ = 48
KVH = 8
HD = 128
FF = 8192
EXPERTS = 2
TOPK = 1
LMAX = 48
MOVE = 2
REQ_DEV = 8
CAP = 6
DEVS = 16
REQS = 128
N_ATTN = 16


def draw_queries(key, part):
    key = jax.random.fold_in(key, 11)
    result = jnp.clip(jax.random.normal(key, (REQS, HQ, HD), jnp.float32), -6.0, 6.0)
    return result.reshape(REQS, HQ * HD).astype(jnp.bfloat16)


def draw_kv_cache(key, part):
    key = jax.random.fold_in(key, 12)
    key_part, value_part = jax.random.split(key)
    values_all = jnp.clip(jax.random.normal(value_part, (REQS, LMAX, KVH * HD), jnp.float32), -6.0, 6.0)
    keys_all = jnp.clip(jax.random.normal(key_part, (REQS, LMAX, KVH, HD), jnp.float32), -6.0, 6.0)
    keys_all = keys_all.reshape(REQS, LMAX, KVH * HD)
    return jnp.concatenate([keys_all, values_all], axis=-1).astype(jnp.bfloat16)


def draw_lengths(key, part):
    key = jax.random.fold_in(key, 13)
    first_key, second_key = jax.random.split(key)
    rank_ids = jnp.arange(REQS, dtype=jnp.int32) // REQ_DEV
    upper = 2 + (LMAX - 2) * (rank_ids + 1) // (REQS // REQ_DEV)
    drawn = jax.random.randint(first_key, (REQS,), 2, upper + 1, dtype=jnp.int32)
    chosen_slot = jax.random.randint(second_key, (), 0, REQ_DEV, dtype=jnp.int32)
    return drawn.at[REQS - REQ_DEV + chosen_slot].set(LMAX).astype(jnp.int32)


def draw_handoff(key, part):
    key = jax.random.fold_in(key, 14)
    row_keys = jax.random.split(key, DEVS)
    orders = jax.vmap(lambda row_key: jax.random.permutation(row_key, REQ_DEV))(row_keys)
    return orders[:, :MOVE].astype(jnp.int32)


def block_levels(stream_key, shape, cuts, least, largest):
    def one(dim, blocks):
        draws = jax.random.uniform(jax.random.fold_in(jax.random.fold_in(stream_key, 6), dim), (blocks,), jnp.float32, least / len(cuts), largest / len(cuts))
        return jnp.repeat(jnp.exp(draws), shape[dim] // blocks).reshape((-1,) + (1,) * (len(shape) - dim - 1))

    gain = one(*cuts[0])
    for cut in cuts[1:]:
        gain = gain * one(*cut)
    return gain


def deal_out(key, own, number, rows, amount, top, reach, skew):
    order = jax.random.permutation(key, amount)
    crowded, usual = shares(amount, rows * top, reach, skew, True), shares(amount, rows * top, reach, skew, False)
    places = jnp.arange(amount)

    def named(sizes, rotation):
        used = int((sizes > 0).sum())
        fixed = max(1, used // 4)
        passed = fixed + (places - fixed + rotation * (used - fixed)) % max(1, amount - fixed)
        return jnp.zeros((amount,), jnp.int32).at[order[jnp.where(places < fixed, places, passed)]].set(jnp.asarray(sizes, jnp.int32))

    sizes = jnp.where(number % 4 == 0, named(crowded, number // 4), named(usual, number - number // 4 - 1))
    mixed = jax.random.permutation(jax.random.fold_in(own, 3), amount)
    source_of, sink = mixed[0:amount // 2 * 2:2], mixed[1:amount // 2 * 2:2]
    margin = jnp.minimum(sizes[source_of] - 1, reach - sizes[sink]) // 2
    margin = jnp.where((source_of == order[0]) | (sink == order[0]) | (sizes[sink] == 0), 0, jnp.maximum(margin, 0))
    passed = jax.random.randint(jax.random.fold_in(own, 4), (amount // 2,), 0, 1 << 20) % (margin + 1)
    sizes = sizes.at[source_of].add(-passed).at[sink].add(passed)
    items = jnp.searchsorted(jnp.cumsum(sizes), jnp.arange(rows * top), side="right").astype(jnp.int32)
    table = items.reshape(top, rows).T
    table = table[jax.random.permutation(jax.random.fold_in(own, 1), rows)]
    rotation = jax.random.randint(jax.random.fold_in(own, 2), (rows, 1), 0, top)
    return jnp.take_along_axis(table, (jnp.arange(top)[None, :] + rotation) % top, axis=1)


def shares(number_of, total, most, skew, full):
    portions = [(1 << 20) // math.isqrt(standing ** skew) + 1 for standing in range(1, number_of + 1)]
    largest = most if full else min(most, max(-(-total // number_of), total * portions[0] // sum(portions)))
    least = 1 if total - largest >= number_of - 1 else 0
    given, spare = [largest] + [least] * (number_of - 1), total - largest - least * (number_of - 1)
    while spare > 0:
        movable = [i for i in range(1, number_of) if given[i] < largest] or [i for i in range(1, number_of) if given[i] < most]
        mass, remaining = sum([portions[i] for i in movable]), spare
        for i in movable:
            extra = min(most - given[i], max(1, remaining * portions[i] // mass), spare)
            given[i] = given[i] + extra
            spare = spare - extra
    return np.array(given)


def normal_values(key, extent, deviation, most, cuts=(), kind=jnp.bfloat16):
    values = deviation * jax.random.normal(key, extent, jnp.float32)
    if cuts:
        values = values * block_levels(key, extent, cuts, -0.22, 0.18)
    return jnp.clip(values, -most, most).astype(kind)


def setup_inputs(seed: int = 0, part: int = 0) -> dict:
    streams_of = jax.random.split(jax.random.key(seed), 11)
    part_splits = jax.random.split(jax.random.fold_in(streams_of[10], part), 11)
    queries = draw_queries(jax.random.fold_in(jax.random.fold_in(streams_of[10], part), 71), part)
    kv_cache = draw_kv_cache(jax.random.fold_in(jax.random.fold_in(streams_of[10], part), 71), part)
    lengths = draw_lengths(jax.random.fold_in(jax.random.fold_in(streams_of[10], part), 71), part)
    handoff = draw_handoff(jax.random.fold_in(jax.random.fold_in(streams_of[10], part), 71), part)
    routes_keys = jax.random.split(jax.random.fold_in(part_splits[4], 1), REQS // REQ_DEV)
    routes_turns = jax.random.permutation(jax.random.fold_in(part_splits[4], 3), REQS // REQ_DEV)
    routes = jax.vmap(lambda own, number: deal_out(jax.random.fold_in(part_splits[4], 2), own, number, REQ_DEV, EXPERTS, TOPK, CAP, 1))(routes_keys, routes_turns).reshape((REQS, TOPK))
    norm_gain = jnp.clip(1.0 + 0.18 * jax.random.normal(streams_of[5], (D,), jnp.float32), 0.099609375, 1.8984375).astype(jnp.bfloat16)
    router = normal_values(streams_of[6], (D, EXPERTS), D ** -0.5, 0.078125)
    gate_proj = normal_values(streams_of[7], (D, EXPERTS * FF), D ** -0.5, 0.078125, ((1, 16),))
    up_proj = normal_values(streams_of[8], (D, EXPERTS * FF), D ** -0.5, 0.078125, ((1, 16),))
    down_proj = normal_values(streams_of[9], (EXPERTS * FF, D), FF ** -0.5, 0.0625, ((0, 16),))
    return {"queries": queries, "kv_cache": kv_cache, "lengths": lengths, "handoff": handoff, "routes": routes, "norm_gain": norm_gain, "router": router, "gate_proj": gate_proj, "up_proj": up_proj, "down_proj": down_proj}


def attend(query_rows, cache_rows, length_rows):
    total_rows = query_rows.shape[0]
    width_kv = KVH * HD
    heads_q = query_rows.reshape(total_rows, KVH, HQ // KVH, HD).astype(jnp.float32)
    keys_all = cache_rows[:, :, :width_kv].reshape(total_rows, LMAX, KVH, HD).astype(jnp.float32)
    values_all = cache_rows[:, :, width_kv:].reshape(total_rows, LMAX, KVH, HD).astype(jnp.float32)
    scores = jnp.einsum('rkgd,rtkd->rkgt', heads_q, keys_all) * HD ** (-0.5)
    visible = jnp.arange(LMAX, dtype=jnp.int32)[None, :] < length_rows[:, None]
    scores = jnp.where(visible[:, None, None, :], scores, -jnp.inf)
    highest = lax.optimization_barrier(jnp.max(scores, axis=-1, keepdims=True))
    weights = jnp.exp(scores - highest)
    weights = (weights / lax.optimization_barrier(jnp.sum(weights, axis=-1, keepdims=True))).astype(jnp.bfloat16)
    mixed_heads = jnp.einsum('rkgt,rtkd->rkgd', weights.astype(jnp.float32), values_all)
    return mixed_heads.reshape(total_rows, HQ * HD).astype(jnp.bfloat16)

def reference(queries, kv_cache, lengths, handoff, routes, norm_gain, router, gate_proj, up_proj, down_proj):
    ranks = handoff.shape[0]
    per_rank = queries.shape[0] // ranks
    rank_ids = jnp.arange(ranks, dtype=jnp.int32)
    partner = jnp.bitwise_xor(rank_ids, ranks // 2)
    slots_out = (rank_ids[:, None] * per_rank + handoff).astype(jnp.int32)
    source = jnp.arange(queries.shape[0], dtype=jnp.int32).at[slots_out.reshape(-1)].set(slots_out[partner].reshape(-1))
    attended = attend(queries[source], kv_cache[source], lengths[source])
    attended_f = attended.astype(jnp.float32)
    scale_rows = lax.rsqrt(lax.optimization_barrier(jnp.mean(attended_f * attended_f, axis=-1, keepdims=True)) + 1e-05)
    normed = (attended_f * scale_rows * norm_gain.astype(jnp.float32)).astype(jnp.bfloat16)
    logits = jnp.dot(normed, router, preferred_element_type=jnp.float32)
    chosen_expert = routes[:, 0]
    chosen_logit = jnp.take_along_axis(logits, routes, axis=1)
    gate_prob = 1.0 / lax.optimization_barrier(jnp.sum(jnp.exp(logits - chosen_logit), axis=1))
    width_dev = EXPERTS * FF // N_ATTN
    shards = FF // width_dev
    output = jnp.zeros(attended_f.shape, jnp.float32)
    for expert in range(EXPERTS):
        gated = jnp.dot(normed, gate_proj[:, expert * FF:(expert + 1) * FF], preferred_element_type=jnp.float32)
        upward = jnp.dot(normed, up_proj[:, expert * FF:(expert + 1) * FF], preferred_element_type=jnp.float32)
        hidden = (jax.nn.silu(gated) * upward).astype(jnp.bfloat16)
        down_rows = down_proj[expert * FF:(expert + 1) * FF]

        def add_shard(running, index, hidden=hidden, down_rows=down_rows):
            start = (index * width_dev).astype(jnp.int32)
            piece_hidden = lax.dynamic_slice_in_dim(hidden, start, width_dev, 1)
            piece_weight = lax.dynamic_slice_in_dim(down_rows, start, width_dev, 0)
            partial_out = jnp.dot(piece_hidden, piece_weight, preferred_element_type=jnp.float32).astype(jnp.bfloat16)
            return (running + lax.optimization_barrier(partial_out).astype(jnp.float32), None)
        summed, unused = lax.scan(add_shard, jnp.zeros(attended_f.shape, jnp.float32), jnp.arange(shards, dtype=jnp.int32))
        output = output + jnp.where((chosen_expert == expert)[:, None], summed, jnp.float32(0.0))
    return (attended_f + gate_prob[:, None] * output).astype(jnp.bfloat16)
```

```python
import functools
import jax
import jax.numpy as jnp
from jax import lax
from jax.experimental import pallas as pl
from jax.experimental.pallas import tpu as pltpu
from jax.sharding import PartitionSpec as P

HQ = 48
KVH = 8
HD = 128
EXPERTS = 2
LMAX = 48
CAP = 6
GROUP = HQ // KVH
MESH = pl.DeviceIdType.MESH
F32 = jnp.float32
BF16 = jnp.bfloat16
RANKS = 16
ROWS = 8
PIECES = 4
COLS = 1024


def layer_kernel(
    lengths, handoff, routes, q_ref, gain_ref, router_ref, kv_hbm, wg_hbm, wu_hbm, wd_hbm, out_ref,
    kv, wg, wu, wd, gathered, x, hidden, codes_out, codes, part, from_core, sum_core, from_first,
    sum_first, from_second, own_sum, sum_second, from_partner, own_rows, own_gate,
    kv_sem, w_sem, code_send, code_recv, g_send, g_recv, r_send, r_recv,
):
    me = lax.axis_index("attn")
    z, y, core = me // 4, (me // 2) % 2, me % 2
    zp, zh = z % 2, z // 2
    sibling, across = me + 1 - 2 * core, me + 2 - 4 * y
    beside = me + 4 - 8 * zp
    partner = me + 8 - 16 * zh
    width = q_ref.shape[1]
    half = width // 2
    chunks = width // COLS

    def remote(src, dst, send, recv, to):
        return pltpu.make_async_remote_copy(
            src_ref=src, dst_ref=dst, send_sem=send, recv_sem=recv,
            device_id={"attn": to}, device_id_type=MESH,
        )

    barrier = pltpu.get_barrier_semaphore()

    def greet(step, carry):
        pl.semaphore_signal(
            barrier, inc=1, device_id={"attn": (me + step) % RANKS}, device_id_type=MESH
        )
        return carry

    lax.fori_loop(1, RANKS, greet, 0)

    kv_copy = pltpu.make_async_copy(kv_hbm, kv, kv_sem)
    kv_copy.start()
    loads = []
    for index, (src, dst) in enumerate(((wg_hbm, wg), (wu_hbm, wu), (wd_hbm, wd))):
        size = dst.shape[0] // PIECES
        for piece in range(PIECES):
            rows = pl.ds(piece * size, size)
            loads.append(pltpu.make_async_copy(src.at[rows], dst.at[rows], w_sem.at[index, piece]))
            loads[-1].start()

    h0, h1 = handoff[0, 0], handoff[0, 1]
    low, high = jnp.minimum(h0, h1), jnp.maximum(h0, h1)

    def order_of(shape):
        row = lax.broadcasted_iota(jnp.int32, shape, 0)
        kept = row + (row >= low).astype(jnp.int32)
        kept = kept + (kept >= high).astype(jnp.int32)
        return jnp.where(row == 6, h0, jnp.where(row == 7, h1, kept))

    slot = lax.broadcasted_iota(jnp.int32, (ROWS, 128), 0)
    place = slot - (slot > h0).astype(jnp.int32) - (slot > h1).astype(jnp.int32)
    source = jnp.where(
        slot == h0, partner * ROWS + 6, jnp.where(slot == h1, partner * ROWS + 7, me * ROWS + place)
    )
    route = jnp.zeros((ROWS, 128), jnp.int32)
    for t in range(ROWS):
        route = jnp.where(slot == t, routes[t, 0], route)
    for e in range(EXPERTS):
        codes_out[e] = jnp.where(route == e, source, -1)
    spot = core * 8 + y * 4 + zp * 2 + zh

    order = order_of((ROWS, ROWS))
    pick = (lax.broadcasted_iota(jnp.int32, (ROWS, ROWS), 1) == order).astype(BF16)
    queries = jnp.dot(pick, q_ref[...], preferred_element_type=F32)
    span = (ROWS, ROWS * LMAX)
    column = lax.broadcasted_iota(jnp.int32, span, 1)
    holder = jnp.zeros(span, jnp.int32)
    for t in range(1, ROWS):
        holder = holder + (column >= t * LMAX).astype(jnp.int32)
    position = column - holder * LMAX
    wide = order_of(span)
    limit = jnp.zeros(span, jnp.int32)
    for t in range(ROWS):
        limit = jnp.where(wide == t, lengths[t], limit)
    visible = jnp.where((holder == wide) & (position < limit), 0.0, -jnp.inf).astype(F32)
    visible = jnp.concatenate([visible] * GROUP, axis=0)
    kv_copy.wait()

    def head(k):
        begin = k * GROUP * HD
        rows = jnp.concatenate(
            [queries[:, begin + g * HD:begin + (g + 1) * HD] for g in range(GROUP)], axis=0
        ).astype(BF16)
        keys = kv[:, :, k * HD:(k + 1) * HD].reshape(ROWS * LMAX, HD)
        values = kv[:, :, (KVH + k) * HD:(KVH + k + 1) * HD].reshape(ROWS * LMAX, HD)
        scores = lax.dot_general(
            rows, keys, (((1,), (1,)), ((), ())), preferred_element_type=F32
        ) * HD ** (-0.5) + visible
        weights = jnp.exp(scores - jnp.max(scores, axis=-1, keepdims=True))
        weights = (weights / jnp.sum(weights, axis=-1, keepdims=True)).astype(BF16)
        return jnp.dot(weights, values, preferred_element_type=F32)

    for k in range(KVH // 2):
        left, right = head(k), head(k + KVH // 2)
        for g in range(GROUP):
            rows = slice(g * ROWS, (g + 1) * ROWS)
            at = (k * GROUP + g) * HD
            gathered[me, :, at:at + HD] = jnp.concatenate([left[rows], right[rows]], axis=0).astype(BF16)

    pl.semaphore_wait(barrier, RANKS - 1)

    UP, DOWN, ACROSS, CORE = range(4)

    def send(kind, block, to):
        return remote(
            gathered.at[block], gathered.at[block], g_send.at[kind, block], g_recv.at[block], to
        )

    def arrived(block):
        send(CORE, block, sibling).wait_recv()

    def code_copy(step):
        to = (me + step) % RANKS
        return remote(
            codes_out.at[to // 8], codes.at[spot], code_send.at[step], code_recv.at[spot], to
        )

    def spread(finish):
        def act(copy):
            copy.wait_send() if finish else copy.start()

        def first(block):
            act(send(ACROSS, block, across))
            act(send(CORE, block, sibling))

        pl.when(z < 3)(lambda: act(send(UP, me, me + 4)))
        pl.when(z > 0)(lambda: act(send(DOWN, me, me - 4)))
        first(me)

        def codes_step(step, carry):
            act(code_copy(step))
            return carry

        lax.fori_loop(1, RANKS, codes_step, 0)

        def from_below(far):
            block = me - 4 * far
            if not finish:
                arrived(block)
            pl.when(z < 3)(lambda: act(send(UP, block, me + 4)))
            first(block)

        def from_above(far):
            block = me + 4 * far
            if not finish:
                arrived(block)
            pl.when(z > 0)(lambda: act(send(DOWN, block, me - 4)))
            first(block)

        def hand_on(block):
            if not finish:
                arrived(block)
            act(send(CORE, block, sibling))

        for far in range(1, 5):
            if far < 4:
                pl.when(z >= far)(functools.partial(from_below, far))
                pl.when(z + far < 4)(functools.partial(from_above, far))
            if far == 1:
                hand_on(across)
            else:
                pl.when(z >= far - 1)(functools.partial(hand_on, across - 4 * (far - 1)))
                pl.when(z + far - 1 < 4)(functools.partial(hand_on, across + 4 * (far - 1)))

    spread(False)
    codes[spot] = codes_out[me // 8]

    def code_wait(step, carry):
        other = (me + step) % RANKS
        there = (other % 2) * 8 + ((other // 2) % 2) * 4 + ((other // 4) % 2) * 2 + other // 8
        remote(
            codes.at[there], codes.at[there], code_send.at[step], code_recv.at[there], sibling
        ).wait_recv()
        return carry

    lax.fori_loop(1, RANKS, code_wait, 0)

    def sibling_wait(chip, carry):
        arrived(chip * 2 + 1 - core)
        return carry

    lax.fori_loop(0, RANKS // 2, sibling_wait, 0)

    def halves(first, second):
        return (
            jnp.concatenate([first[:ROWS], second[:ROWS]], axis=0),
            jnp.concatenate([first[ROWS:], second[ROWS:]], axis=0),
        )

    def norm(left, right):
        total = jnp.sum(left * left, axis=-1, keepdims=True) + jnp.sum(
            right * right, axis=-1, keepdims=True
        )
        scale = lax.rsqrt(total / width + 1e-05)
        return (
            (left * scale * gain_ref[:, :half].astype(F32)).astype(BF16),
            (right * scale * gain_ref[:, half:].astype(F32)).astype(BF16),
        )

    def norm_step(chip, carry):
        left, right = halves(gathered[2 * chip].astype(F32), gathered[2 * chip + 1].astype(F32))
        left, right = norm(left, right)
        rows = pl.ds(pl.multiple_of(chip * 16, 16), 16)
        x[rows, :half] = left
        x[rows, half:] = right
        return carry

    lax.fori_loop(0, RANKS // 2, norm_step, 0)

    for copy in loads[:2 * PIECES]:
        copy.wait()

    def up_step(tile, carry):
        columns = pl.ds(pl.multiple_of(tile * 256, 256), 256)
        gated = jnp.dot(x[...], wg[:, columns], preferred_element_type=F32)
        upward = jnp.dot(x[...], wu[:, columns], preferred_element_type=F32)
        hidden[:, columns] = (gated / (1.0 + jnp.exp(-gated)) * upward).astype(BF16)
        return carry

    lax.fori_loop(0, wg.shape[1] // 256, up_step, 0)

    chosen = codes[...].reshape(RANKS * ROWS, 128)
    select = (lax.broadcasted_iota(jnp.int32, chosen.shape, 1) == chosen).astype(BF16)
    hidden[...] = jnp.dot(select, hidden[...], preferred_element_type=F32).astype(BF16)
    for copy in loads[2 * PIECES:]:
        copy.wait()

    def core_copy(j):
        return remote(
            part.at[j, 1 - core], from_core.at[j], r_send.at[0, j], r_recv.at[0, j], sibling
        )

    def first_copy(j):
        if j % 2 == 0:
            return remote(
                sum_core.at[j, 1 - y], from_first.at[j], r_send.at[1, j], r_recv.at[1, j], across
            )
        return remote(
            sum_core.at[j, :, 1 - zp], from_first.at[j], r_send.at[1, j], r_recv.at[1, j], beside
        )

    def second_copy(j):
        if j % 2 == 0:
            return remote(
                sum_first.at[j, 1 - zp], from_second.at[j], r_send.at[2, j], r_recv.at[2, j], beside
            )
        return remote(
            sum_first.at[j, 1 - y], from_second.at[j], r_send.at[2, j], r_recv.at[2, j], across
        )

    def partner_copy(j):
        return remote(
            sum_second.at[j], from_partner.at[j], r_send.at[3, j], r_recv.at[3, j], partner
        )

    def down(j):
        part[j] = jnp.dot(
            hidden[...], wd[:, j * COLS:(j + 1) * COLS], preferred_element_type=F32
        ).astype(BF16).reshape(2, 2, 2, 16, COLS)
        core_copy(j).start()

    def add_core(j):
        core_copy(j).wait_recv()
        sum_core[j] = (part[j, core].astype(F32) + from_core[j].astype(F32)).astype(BF16)
        first_copy(j).start()

    def add_first(j):
        first_copy(j).wait_recv()
        mine = sum_core[j, y] if j % 2 == 0 else sum_core[j, :, zp]
        sum_first[j] = (mine.astype(F32) + from_first[j].astype(F32)).astype(BF16)
        second_copy(j).start()

    def add_second(j):
        second_copy(j).wait_recv()
        mine = sum_first[j, zp] if j % 2 == 0 else sum_first[j, y]
        total = mine.astype(F32) + from_second[j].astype(F32)
        upper = zh == 1
        own_sum[j] = jnp.where(upper, total[ROWS:], total[:ROWS])
        other = jnp.where(upper, total[:ROWS], total[ROWS:])
        sum_second[j] = jnp.concatenate(
            [other[:, :COLS // 2], other[:, COLS // 2:]], axis=0
        ).astype(BF16)
        partner_copy(j).start()

    def own():
        near = jnp.where(
            slot == h0, ROWS + 6, jnp.where(slot == h1, ROWS + 7, place)
        )[:, :2 * ROWS]
        take = (lax.broadcasted_iota(jnp.int32, near.shape, 1) == near).astype(BF16)
        left, right = halves(gathered[me].astype(F32), gathered[partner].astype(F32))
        left = jnp.dot(take, left.astype(BF16), preferred_element_type=F32)
        right = jnp.dot(take, right.astype(BF16), preferred_element_type=F32)
        own_rows[:, :half] = left
        own_rows[:, half:] = right
        left, right = norm(left, right)
        logits = []
        for e in range(EXPERTS):
            weight = router_ref[e:e + 1, :].astype(F32)
            logits.append(
                jnp.sum(left.astype(F32) * weight[:, :half], axis=-1, keepdims=True)
                + jnp.sum(right.astype(F32) * weight[:, half:], axis=-1, keepdims=True)
            )
        chosen_logit = jnp.where(route[:, :1] == 0, logits[0], logits[1])
        odds = jnp.exp(logits[0] - chosen_logit) + jnp.exp(logits[1] - chosen_logit)
        own_gate[...] = jnp.broadcast_to(1.0 / odds, own_gate.shape)

    def finish(j):
        partner_copy(j).wait_recv()
        other = from_partner[j].astype(F32)
        other = jnp.concatenate([other[:ROWS], other[ROWS:]], axis=1)
        columns = slice(j * COLS, (j + 1) * COLS)
        out_ref[:, columns] = (
            own_rows[:, columns] + own_gate[:, :1] * (own_sum[j] + other)
        ).astype(BF16)

    for step in range(chunks + 4):
        if step < chunks:
            down(step)
        if step == 1:
            own()
        for late, act in enumerate((add_core, add_first, add_second, finish)):
            if 0 <= step - late - 1 < chunks:
                act(step - late - 1)

    spread(True)
    for j in range(chunks):
        for copy in (core_copy, first_copy, second_copy, partner_copy):
            copy(j).wait_send()


def fused(queries, kv_cache, lengths, handoff, routes, norm_gain, router, gate_proj, up_proj, down_proj):
    width = queries.shape[1]
    inner = gate_proj.shape[1]
    chunks = width // COLS
    smem = pl.BlockSpec(memory_space=pltpu.SMEM)
    vmem = pl.BlockSpec(memory_space=pltpu.VMEM)
    hbm = pl.BlockSpec(memory_space=pl.ANY)
    dma = pltpu.SemaphoreType.DMA
    return pl.pallas_call(
        layer_kernel,
        out_shape=jax.ShapeDtypeStruct(queries.shape, BF16),
        in_specs=[smem, smem, smem, vmem, vmem, vmem, hbm, hbm, hbm, hbm],
        out_specs=vmem,
        scratch_shapes=[
            pltpu.VMEM(kv_cache.shape, BF16),
            pltpu.VMEM(gate_proj.shape, BF16),
            pltpu.VMEM(up_proj.shape, BF16),
            pltpu.VMEM(down_proj.shape, BF16),
            pltpu.VMEM((RANKS, 2 * ROWS, width // 2), BF16),
            pltpu.VMEM((RANKS * ROWS, width), BF16),
            pltpu.VMEM((RANKS * ROWS, inner), BF16),
            pltpu.VMEM((EXPERTS, ROWS, 128), jnp.int32),
            pltpu.VMEM((RANKS, ROWS, 128), jnp.int32),
            pltpu.VMEM((chunks, 2, 2, 2, 16, COLS), BF16),
            pltpu.VMEM((chunks, 2, 2, 16, COLS), BF16),
            pltpu.VMEM((chunks, 2, 2, 16, COLS), BF16),
            pltpu.VMEM((chunks, 2, 16, COLS), BF16),
            pltpu.VMEM((chunks, 2, 16, COLS), BF16),
            pltpu.VMEM((chunks, 16, COLS), BF16),
            pltpu.VMEM((chunks, ROWS, COLS), F32),
            pltpu.VMEM((chunks, 16, COLS // 2), BF16),
            pltpu.VMEM((chunks, 16, COLS // 2), BF16),
            pltpu.VMEM((ROWS, width), F32),
            pltpu.VMEM((ROWS, 128), F32),
            dma,
            dma((3, PIECES)),
            dma((RANKS,)),
            dma((RANKS,)),
            dma((4, RANKS)),
            dma((RANKS,)),
            dma((4, chunks)),
            dma((4, chunks)),
        ],
        compiler_params=pltpu.CompilerParams(
            collective_id=0, has_side_effects=True, vmem_limit_bytes=60 * 1024 * 1024
        ),
        cost_estimate=pl.CostEstimate(
            flops=6 * RANKS * ROWS * width * inner,
            bytes_accessed=6 * width * inner,
            transcendentals=0,
        ),
    )(
        lengths, handoff, routes, queries, norm_gain[None, :], router.T, kv_cache,
        gate_proj, up_proj, down_proj,
    )


def partner(array, axis, distance):
    return lax.ppermute(array, axis, [(i, i ^ 1 << distance) for i in range(lax.axis_size(axis))])


def attend(query_rows, cache_rows, length_rows):
    total_rows = query_rows.shape[0]
    width_kv = KVH * HD
    heads_q = query_rows.reshape(total_rows, KVH, HQ // KVH, HD)
    keys_all = cache_rows[:, :, :width_kv].reshape(total_rows, LMAX, KVH, HD)
    values_all = cache_rows[:, :, width_kv:].reshape(total_rows, LMAX, KVH, HD)
    scores = jnp.einsum(
        "rkgd,rtkd->rkgt", heads_q, keys_all, preferred_element_type=jnp.float32
    ) * HD ** (-0.5)
    visible = jnp.arange(LMAX, dtype=jnp.int32)[None, :] < length_rows[:, None]
    scores = jnp.where(visible[:, None, None, :], scores, -jnp.inf)
    highest = jnp.max(scores, axis=-1, keepdims=True)
    weights = jnp.exp(scores - highest)
    weights = (weights / jnp.sum(weights, axis=-1, keepdims=True)).astype(jnp.bfloat16)
    mixed_heads = jnp.einsum(
        "rkgt,rtkd->rkgd", weights, values_all, preferred_element_type=jnp.float32
    )
    return mixed_heads.reshape(total_rows, HQ * HD).astype(jnp.bfloat16)


def body(
    queries, kv_cache, lengths, handoff, routes, norm_gain, router, gate_proj, up_proj, down_proj
):
    ranks = lax.axis_size("attn")
    if ranks == RANKS and queries.shape[0] == ROWS:
        return fused(
            queries, kv_cache, lengths, handoff, routes, norm_gain, router,
            gate_proj, up_proj, down_proj,
        )
    picks = handoff[0]
    highest_bit = ranks.bit_length() - 2
    attended = attend(queries, kv_cache, lengths)
    attended = attended.at[picks].set(partner(attended[picks], "attn", highest_bit))
    attended_f = attended.astype(jnp.float32)
    scale_rows = lax.rsqrt(jnp.mean(attended_f * attended_f, axis=-1, keepdims=True) + 1e-05)
    normed = (attended_f * scale_rows * norm_gain.astype(jnp.float32)).astype(jnp.bfloat16)
    logits = jnp.dot(normed, router, preferred_element_type=jnp.float32)
    chosen_logit = jnp.take_along_axis(logits, routes, axis=1)
    gate_prob = 1.0 / jnp.sum(jnp.exp(logits - chosen_logit), axis=1)
    chosen_expert = routes[:, 0]
    row_order = jnp.arange(chosen_expert.shape[0], dtype=jnp.int32)
    earlier = (chosen_expert[:, None] == chosen_expert[None, :]) & (
        row_order[None, :] < row_order[:, None]
    )
    slot_index = jnp.sum(earlier.astype(jnp.int32), axis=1)
    target = chosen_expert * CAP + slot_index
    selector = (jnp.arange(EXPERTS * CAP, dtype=jnp.int32)[:, None] == target[None, :]).astype(
        jnp.bfloat16
    )
    width = normed.shape[1]
    dispatch = (
        jnp.dot(selector, normed, preferred_element_type=jnp.float32)
        .astype(jnp.bfloat16)
        .reshape(EXPERTS, CAP, width)
    )
    group_size = ranks // EXPERTS
    mine = lax.axis_index("attn") // group_size
    own_rows = lax.dynamic_index_in_dim(
        lax.all_gather(dispatch[None], "attn", axis=0, tiled=True), mine, 1, keepdims=False
    )
    flat = own_rows.reshape(-1, width)
    gated = jnp.dot(flat, gate_proj, preferred_element_type=jnp.float32)
    upward = jnp.dot(flat, up_proj, preferred_element_type=jnp.float32)
    hidden = (jax.nn.silu(gated) * upward).astype(jnp.bfloat16)
    partial_out = jnp.dot(hidden, down_proj, preferred_element_type=jnp.float32).astype(
        jnp.bfloat16
    )
    partials = partial_out.reshape(own_rows.shape)
    received = lax.all_to_all(partials, "attn", split_axis=0, concat_axis=0, tiled=True)
    summed = received.astype(jnp.float32).reshape(EXPERTS, group_size, CAP, width).sum(axis=1)
    expert_value = jnp.take(summed.reshape(EXPERTS * CAP, width), target, axis=0)
    return (attended_f + gate_prob[:, None] * expert_value).astype(jnp.bfloat16)


def solution(mesh):
    return jax.shard_map(
        body,
        mesh=mesh,
        in_specs=(
            P(("groups", "attn"), None),
            P(("groups", "attn"), None, None),
            P(("groups", "attn")),
            P(("groups", "attn"), None),
            P(("groups", "attn"), None),
            P(),
            P(),
            P(None, "attn"),
            P(None, "attn"),
            P("attn", None),
        ),
        out_specs=P(("groups", "attn"), None),
        check_vma=False,
    )
```

```python
import functools
import jax
import jax.numpy as jnp
from jax import lax
from jax.experimental import pallas as pl
from jax.experimental.pallas import tpu as pltpu
from jax.sharding import PartitionSpec as P

HQ = 48
KVH = 8
HD = 128
EXPERTS = 2
LMAX = 48
CAP = 6
GROUP = HQ // KVH
MESH = pl.DeviceIdType.MESH
F32 = jnp.float32
BF16 = jnp.bfloat16
RANKS = 16
ROWS = 8
PIECES = 8
FIRST = 8
EACH = 2
LAGS = (2, 5, 8, 11)
COLS = 1024


def layer_kernel(
    lengths, handoff, routes, q_ref, gain_ref, router_ref, kv_hbm, wg_hbm, wu_hbm, wd_hbm, out_ref,
    kv, wg, wu, wd, gathered, x, hidden, part, from_core, sum_core, from_first,
    sum_first, from_second, own_sum, sum_second, from_partner, own_rows, own_gate,
    kv_sem, w_sem, g_send, g_recv, r_send, r_recv,
):
    me = lax.axis_index("attn")
    z, y, core = me // 4, (me // 2) % 2, me % 2
    zp, zh = z % 2, z // 2
    sibling, across = me + 1 - 2 * core, me + 2 - 4 * y
    beside = me + 4 - 8 * zp
    partner = me + 8 - 16 * zh
    width = q_ref.shape[1]
    half = width // 2
    chunks = width // COLS

    def remote(src, dst, send, recv, to):
        return pltpu.make_async_remote_copy(
            src_ref=src, dst_ref=dst, send_sem=send, recv_sem=recv,
            device_id={"attn": to}, device_id_type=MESH,
        )

    barrier = pltpu.get_barrier_semaphore()

    def greet(to):
        pl.semaphore_signal(barrier, inc=1, device_id={"attn": to}, device_id_type=MESH)

    pl.when(z < 3)(lambda: greet(me + 4))
    pl.when(z > 0)(lambda: greet(me - 4))
    for to in (across, sibling, partner):
        greet(to)

    kv_copy = pltpu.make_async_copy(kv_hbm, kv, kv_sem)
    kv_copy.start()
    loads = []
    for index, (src, dst) in enumerate(((wg_hbm, wg), (wu_hbm, wu), (wd_hbm, wd))):
        size = dst.shape[0] // PIECES
        for piece in range(PIECES):
            rows = pl.ds(piece * size, size)
            loads.append(pltpu.make_async_copy(src.at[rows], dst.at[rows], w_sem.at[index, piece]))

    started = [0]

    def load(amount):
        for copy in loads[started[0]:started[0] + amount]:
            copy.start()
        started[0] += amount

    load(FIRST)

    h0, h1 = handoff[0, 0], handoff[0, 1]
    low, high = jnp.minimum(h0, h1), jnp.maximum(h0, h1)

    def order_of(shape):
        row = lax.broadcasted_iota(jnp.int32, shape, 0)
        kept = row + (row >= low).astype(jnp.int32)
        kept = kept + (kept >= high).astype(jnp.int32)
        return jnp.where(row == 6, h0, jnp.where(row == 7, h1, kept))

    slot = lax.broadcasted_iota(jnp.int32, (ROWS, 128), 0)
    place = slot - (slot > h0).astype(jnp.int32) - (slot > h1).astype(jnp.int32)
    source = jnp.where(
        slot == h0, partner * ROWS + 6, jnp.where(slot == h1, partner * ROWS + 7, me * ROWS + place)
    )
    route = jnp.zeros((ROWS, 128), jnp.int32)
    for t in range(ROWS):
        route = jnp.where(slot == t, routes[t], route)
    gathered[me, :, half:] = jnp.concatenate(
        [jnp.where(route == e, source, -1).astype(F32) for e in range(EXPERTS)], axis=0
    ).astype(BF16)

    order = order_of((ROWS, ROWS))
    pick = (lax.broadcasted_iota(jnp.int32, (ROWS, ROWS), 1) == order).astype(BF16)
    queries = jnp.dot(pick, q_ref[...], preferred_element_type=F32)
    span = (ROWS, ROWS * LMAX)
    column = lax.broadcasted_iota(jnp.int32, span, 1)
    holder = jnp.zeros(span, jnp.int32)
    for t in range(1, ROWS):
        holder = holder + (column >= t * LMAX).astype(jnp.int32)
    position = column - holder * LMAX
    wide = order_of(span)
    limit = jnp.zeros(span, jnp.int32)
    for t in range(ROWS):
        limit = jnp.where(wide == t, lengths[t], limit)
    visible = jnp.where((holder == wide) & (position < limit), 0.0, -jnp.inf).astype(F32)
    visible = jnp.concatenate([visible] * GROUP, axis=0)
    kv_copy.wait()

    def head(k):
        begin = k * GROUP * HD
        rows = jnp.concatenate(
            [queries[:, begin + g * HD:begin + (g + 1) * HD] for g in range(GROUP)], axis=0
        ).astype(BF16)
        keys = kv[:, :, k * HD:(k + 1) * HD].reshape(ROWS * LMAX, HD)
        values = kv[:, :, (KVH + k) * HD:(KVH + k + 1) * HD].reshape(ROWS * LMAX, HD)
        scores = lax.dot_general(
            rows, keys, (((1,), (1,)), ((), ())), preferred_element_type=F32
        ) * HD ** (-0.5) + visible
        weights = jnp.exp(scores - jnp.max(scores, axis=-1, keepdims=True))
        weights = (weights / jnp.sum(weights, axis=-1, keepdims=True)).astype(BF16)
        return jnp.dot(weights, values, preferred_element_type=F32)

    for k in range(KVH // 2):
        left, right = head(k), head(k + KVH // 2)
        for g in range(GROUP):
            rows = slice(g * ROWS, (g + 1) * ROWS)
            at = (k * GROUP + g) * HD
            gathered[me, :, at:at + HD] = jnp.concatenate([left[rows], right[rows]], axis=0).astype(BF16)

    pl.semaphore_wait(barrier, 3 + (z < 3).astype(jnp.int32) + (z > 0).astype(jnp.int32))

    UP, DOWN, ACROSS, CORE = range(4)

    def send(kind, block, to):
        return remote(
            gathered.at[block], gathered.at[block], g_send.at[kind, block], g_recv.at[block], to
        )

    def arrived(block):
        send(CORE, block, sibling).wait_recv()

    def spread(finish):
        def act(copy):
            copy.wait_send() if finish else copy.start()

        def first(block):
            act(send(ACROSS, block, across))
            act(send(CORE, block, sibling))

        pl.when(z < 3)(lambda: act(send(UP, me, me + 4)))
        pl.when(z > 0)(lambda: act(send(DOWN, me, me - 4)))
        first(me)

        def from_below(far):
            block = me - 4 * far
            if not finish:
                arrived(block)
            pl.when(z < 3)(lambda: act(send(UP, block, me + 4)))
            first(block)

        def from_above(far):
            block = me + 4 * far
            if not finish:
                arrived(block)
            pl.when(z > 0)(lambda: act(send(DOWN, block, me - 4)))
            first(block)

        def hand_on(block):
            if not finish:
                arrived(block)
            act(send(CORE, block, sibling))

        for far in range(1, 5):
            if not finish:
                load(EACH)
            if far < 4:
                pl.when(z >= far)(functools.partial(from_below, far))
                pl.when(z + far < 4)(functools.partial(from_above, far))
            if far == 1:
                hand_on(across)
            else:
                pl.when(z >= far - 1)(functools.partial(hand_on, across - 4 * (far - 1)))
                pl.when(z + far - 1 < 4)(functools.partial(hand_on, across + 4 * (far - 1)))

    spread(False)
    def sibling_wait(chip, carry):
        arrived(chip * 2 + 1 - core)
        return carry

    lax.fori_loop(0, RANKS // 2, sibling_wait, 0)

    load(len(loads) - started[0])

    def halves(first, second):
        return (
            jnp.concatenate([first[:ROWS], second[:ROWS]], axis=0),
            jnp.concatenate([first[ROWS:], second[ROWS:]], axis=0),
        )

    def norm(left, right):
        total = jnp.sum(left * left, axis=-1, keepdims=True) + jnp.sum(
            right * right, axis=-1, keepdims=True
        )
        scale = lax.rsqrt(total / width + 1e-05)
        return (
            (left * scale * gain_ref[pl.ds(0, half)].astype(F32)[None, :]).astype(BF16),
            (right * scale * gain_ref[pl.ds(half, half)].astype(F32)[None, :]).astype(BF16),
        )

    def norm_step(chip, carry):
        left, right = halves(gathered[2 * chip, :, :half].astype(F32), gathered[2 * chip + 1, :, :half].astype(F32))
        left, right = norm(left, right)
        rows = pl.ds(pl.multiple_of(chip * 16, 16), 16)
        x[rows, :half] = left
        x[rows, half:] = right
        return carry

    lax.fori_loop(0, RANKS // 2, norm_step, 0)

    for copy in loads[:2 * PIECES]:
        copy.wait()

    def up_step(tile, carry):
        columns = pl.ds(pl.multiple_of(tile * 256, 256), 256)
        gated = jnp.dot(x[...], wg[:, columns], preferred_element_type=F32)
        upward = jnp.dot(x[...], wu[:, columns], preferred_element_type=F32)
        hidden[:, columns] = (gated / (1.0 + jnp.exp(-gated)) * upward).astype(BF16)
        return carry

    lax.fori_loop(0, wg.shape[1] // 256, up_step, 0)

    chosen = []
    for spot in range(RANKS):
        rank = (spot % 2 * 2 + spot // 2 % 2) * 4 + spot // 4 % 2 * 2 + spot // 8
        codes = gathered[rank, :, half:].astype(F32)
        chosen.append(jnp.where(zh == 0, codes[:ROWS], codes[ROWS:]))
    chosen = jnp.concatenate(chosen, axis=0)
    lane = lax.broadcasted_iota(jnp.int32, chosen.shape, 1).astype(F32)
    select = (lane == chosen).astype(BF16)
    hidden[...] = jnp.dot(select, hidden[...], preferred_element_type=F32).astype(BF16)
    for copy in loads[2 * PIECES:]:
        copy.wait()

    def core_copy(j):
        return remote(
            part.at[j, 1 - core], from_core.at[j], r_send.at[0, j], r_recv.at[0, j], sibling
        )

    def first_copy(j):
        if j % 2 == 0:
            return remote(
                sum_core.at[j, 1 - y], from_first.at[j], r_send.at[1, j], r_recv.at[1, j], across
            )
        return remote(
            sum_core.at[j, :, 1 - zp], from_first.at[j], r_send.at[1, j], r_recv.at[1, j], beside
        )

    def second_copy(j):
        if j % 2 == 0:
            return remote(
                sum_first.at[j, 1 - zp], from_second.at[j], r_send.at[2, j], r_recv.at[2, j], beside
            )
        return remote(
            sum_first.at[j, 1 - y], from_second.at[j], r_send.at[2, j], r_recv.at[2, j], across
        )

    def partner_copy(j):
        return remote(
            sum_second.at[j], from_partner.at[j], r_send.at[3, j], r_recv.at[3, j], partner
        )

    def down(j):
        part[j] = jnp.dot(
            hidden[...], wd[:, j * COLS:(j + 1) * COLS], preferred_element_type=F32
        ).astype(BF16).reshape(2, 2, 2, 16, COLS)
        core_copy(j).start()

    def add_core(j):
        core_copy(j).wait_recv()
        sum_core[j] = (part[j, core].astype(F32) + from_core[j].astype(F32)).astype(BF16)
        first_copy(j).start()

    def add_first(j):
        first_copy(j).wait_recv()
        mine = sum_core[j, y] if j % 2 == 0 else sum_core[j, :, zp]
        sum_first[j] = (mine.astype(F32) + from_first[j].astype(F32)).astype(BF16)
        second_copy(j).start()

    def add_second(j):
        second_copy(j).wait_recv()
        mine = sum_first[j, zp] if j % 2 == 0 else sum_first[j, y]
        total = mine.astype(F32) + from_second[j].astype(F32)
        upper = zh == 1
        own_sum[j] = jnp.where(upper, total[ROWS:], total[:ROWS])
        other = jnp.where(upper, total[:ROWS], total[ROWS:])
        sum_second[j] = jnp.concatenate(
            [other[:, :COLS // 2], other[:, COLS // 2:]], axis=0
        ).astype(BF16)
        partner_copy(j).start()

    def own():
        near = jnp.where(
            slot == h0, ROWS + 6, jnp.where(slot == h1, ROWS + 7, place)
        )[:, :2 * ROWS]
        take = (lax.broadcasted_iota(jnp.int32, near.shape, 1) == near).astype(BF16)
        left, right = halves(gathered[me, :, :half].astype(F32), gathered[partner, :, :half].astype(F32))
        left = jnp.dot(take, left.astype(BF16), preferred_element_type=F32)
        right = jnp.dot(take, right.astype(BF16), preferred_element_type=F32)
        own_rows[:, :half] = left
        own_rows[:, half:] = right
        left, right = norm(left, right)
        logits = []
        for e in range(EXPERTS):
            weight = router_ref[e:e + 1, :].astype(F32)
            logits.append(
                jnp.sum(left.astype(F32) * weight[:, :half], axis=-1, keepdims=True)
                + jnp.sum(right.astype(F32) * weight[:, half:], axis=-1, keepdims=True)
            )
        chosen_logit = jnp.where(route[:, :1] == 0, logits[0], logits[1])
        odds = jnp.exp(logits[0] - chosen_logit) + jnp.exp(logits[1] - chosen_logit)
        own_gate[...] = jnp.broadcast_to(1.0 / odds, own_gate.shape)

    def finish(j):
        partner_copy(j).wait_recv()
        other = from_partner[j].astype(F32)
        other = jnp.concatenate([other[:ROWS], other[ROWS:]], axis=1)
        columns = slice(j * COLS, (j + 1) * COLS)
        out_ref[:, columns] = (
            own_rows[:, columns] + own_gate[:, :1] * (own_sum[j] + other)
        ).astype(BF16)

    for step in range(chunks + LAGS[-1]):
        if step < chunks:
            down(step)
        if step == chunks - 1:
            own()
        for late, act in zip(LAGS, (add_core, add_first, add_second, finish)):
            if 0 <= step - late < chunks:
                act(step - late)

    spread(True)
    for j in range(chunks):
        for copy in (core_copy, first_copy, second_copy, partner_copy):
            copy(j).wait_send()


def fused(queries, kv_cache, lengths, handoff, routes, norm_gain, router, gate_proj, up_proj, down_proj):
    width = queries.shape[1]
    inner = gate_proj.shape[1]
    chunks = width // COLS
    smem = pl.BlockSpec(memory_space=pltpu.SMEM)
    vmem = pl.BlockSpec(memory_space=pltpu.VMEM)
    hbm = pl.BlockSpec(memory_space=pl.ANY)
    dma = pltpu.SemaphoreType.DMA
    return pl.pallas_call(
        layer_kernel,
        out_shape=jax.ShapeDtypeStruct(queries.shape, BF16),
        in_specs=[smem, smem, smem, vmem, vmem, vmem, hbm, hbm, hbm, hbm],
        out_specs=vmem,
        scratch_shapes=[
            pltpu.VMEM(kv_cache.shape, BF16),
            pltpu.VMEM(gate_proj.shape, BF16),
            pltpu.VMEM(up_proj.shape, BF16),
            pltpu.VMEM(down_proj.shape, BF16),
            pltpu.VMEM((RANKS, 2 * ROWS, width // 2 + 128), BF16),
            pltpu.VMEM((RANKS * ROWS, width), BF16),
            pltpu.VMEM((RANKS * ROWS, inner), BF16),
            pltpu.VMEM((chunks, 2, 2, 2, 16, COLS), BF16),
            pltpu.VMEM((chunks, 2, 2, 16, COLS), BF16),
            pltpu.VMEM((chunks, 2, 2, 16, COLS), BF16),
            pltpu.VMEM((chunks, 2, 16, COLS), BF16),
            pltpu.VMEM((chunks, 2, 16, COLS), BF16),
            pltpu.VMEM((chunks, 16, COLS), BF16),
            pltpu.VMEM((chunks, ROWS, COLS), F32),
            pltpu.VMEM((chunks, 16, COLS // 2), BF16),
            pltpu.VMEM((chunks, 16, COLS // 2), BF16),
            pltpu.VMEM((ROWS, width), F32),
            pltpu.VMEM((ROWS, 128), F32),
            dma,
            dma((3, PIECES)),
            dma((4, RANKS)),
            dma((RANKS,)),
            dma((4, chunks)),
            dma((4, chunks)),
        ],
        compiler_params=pltpu.CompilerParams(
            collective_id=0, has_side_effects=True, vmem_limit_bytes=60 * 1024 * 1024
        ),
        cost_estimate=pl.CostEstimate(
            flops=6 * RANKS * ROWS * width * inner,
            bytes_accessed=6 * width * inner,
            transcendentals=0,
        ),
    )(
        lengths, handoff, routes[:, 0], queries, norm_gain, router.T, kv_cache,
        gate_proj, up_proj, down_proj,
    )


def partner(array, axis, distance):
    return lax.ppermute(array, axis, [(i, i ^ 1 << distance) for i in range(lax.axis_size(axis))])


def attend(query_rows, cache_rows, length_rows):
    total_rows = query_rows.shape[0]
    width_kv = KVH * HD
    heads_q = query_rows.reshape(total_rows, KVH, HQ // KVH, HD)
    keys_all = cache_rows[:, :, :width_kv].reshape(total_rows, LMAX, KVH, HD)
    values_all = cache_rows[:, :, width_kv:].reshape(total_rows, LMAX, KVH, HD)
    scores = jnp.einsum(
        "rkgd,rtkd->rkgt", heads_q, keys_all, preferred_element_type=jnp.float32
    ) * HD ** (-0.5)
    visible = jnp.arange(LMAX, dtype=jnp.int32)[None, :] < length_rows[:, None]
    scores = jnp.where(visible[:, None, None, :], scores, -jnp.inf)
    highest = jnp.max(scores, axis=-1, keepdims=True)
    weights = jnp.exp(scores - highest)
    weights = (weights / jnp.sum(weights, axis=-1, keepdims=True)).astype(jnp.bfloat16)
    mixed_heads = jnp.einsum(
        "rkgt,rtkd->rkgd", weights, values_all, preferred_element_type=jnp.float32
    )
    return mixed_heads.reshape(total_rows, HQ * HD).astype(jnp.bfloat16)


def body(
    queries, kv_cache, lengths, handoff, routes, norm_gain, router, gate_proj, up_proj, down_proj
):
    ranks = lax.axis_size("attn")
    if ranks == RANKS and queries.shape[0] == ROWS:
        return fused(
            queries, kv_cache, lengths, handoff, routes, norm_gain, router,
            gate_proj, up_proj, down_proj,
        )
    picks = handoff[0]
    highest_bit = ranks.bit_length() - 2
    attended = attend(queries, kv_cache, lengths)
    attended = attended.at[picks].set(partner(attended[picks], "attn", highest_bit))
    attended_f = attended.astype(jnp.float32)
    scale_rows = lax.rsqrt(jnp.mean(attended_f * attended_f, axis=-1, keepdims=True) + 1e-05)
    normed = (attended_f * scale_rows * norm_gain.astype(jnp.float32)).astype(jnp.bfloat16)
    logits = jnp.dot(normed, router, preferred_element_type=jnp.float32)
    chosen_logit = jnp.take_along_axis(logits, routes, axis=1)
    gate_prob = 1.0 / jnp.sum(jnp.exp(logits - chosen_logit), axis=1)
    chosen_expert = routes[:, 0]
    row_order = jnp.arange(chosen_expert.shape[0], dtype=jnp.int32)
    earlier = (chosen_expert[:, None] == chosen_expert[None, :]) & (
        row_order[None, :] < row_order[:, None]
    )
    slot_index = jnp.sum(earlier.astype(jnp.int32), axis=1)
    target = chosen_expert * CAP + slot_index
    selector = (jnp.arange(EXPERTS * CAP, dtype=jnp.int32)[:, None] == target[None, :]).astype(
        jnp.bfloat16
    )
    width = normed.shape[1]
    dispatch = (
        jnp.dot(selector, normed, preferred_element_type=jnp.float32)
        .astype(jnp.bfloat16)
        .reshape(EXPERTS, CAP, width)
    )
    group_size = ranks // EXPERTS
    mine = lax.axis_index("attn") // group_size
    own_rows = lax.dynamic_index_in_dim(
        lax.all_gather(dispatch[None], "attn", axis=0, tiled=True), mine, 1, keepdims=False
    )
    flat = own_rows.reshape(-1, width)
    gated = jnp.dot(flat, gate_proj, preferred_element_type=jnp.float32)
    upward = jnp.dot(flat, up_proj, preferred_element_type=jnp.float32)
    hidden = (jax.nn.silu(gated) * upward).astype(jnp.bfloat16)
    partial_out = jnp.dot(hidden, down_proj, preferred_element_type=jnp.float32).astype(
        jnp.bfloat16
    )
    partials = partial_out.reshape(own_rows.shape)
    received = lax.all_to_all(partials, "attn", split_axis=0, concat_axis=0, tiled=True)
    summed = received.astype(jnp.float32).reshape(EXPERTS, group_size, CAP, width).sum(axis=1)
    expert_value = jnp.take(summed.reshape(EXPERTS * CAP, width), target, axis=0)
    return (attended_f + gate_prob[:, None] * expert_value).astype(jnp.bfloat16)


def solution(mesh):
    return jax.shard_map(
        body,
        mesh=mesh,
        in_specs=(
            P(("groups", "attn"), None),
            P(("groups", "attn"), None, None),
            P(("groups", "attn")),
            P(("groups", "attn"), None),
            P(("groups", "attn"), None),
            P(),
            P(),
            P(None, "attn"),
            P(None, "attn"),
            P("attn", None),
        ),
        out_specs=P(("groups", "attn"), None),
        check_vma=False,
    )
```

```python
import functools
import jax
import jax.numpy as jnp
from jax import lax
from jax.experimental import pallas as pl
from jax.experimental.pallas import tpu as pltpu
from jax.sharding import PartitionSpec as P

HQ = 48
KVH = 8
HD = 128
EXPERTS = 2
LMAX = 48
CAP = 6
GROUP = HQ // KVH
MESH = pl.DeviceIdType.MESH
F32 = jnp.float32
BF16 = jnp.bfloat16
RANKS = 16
ROWS = 8
PIECES = 8
FIRST = 24
PARTS = 2
LAGS = (2, 5, 8, 11)
COLS = 1024


def layer_kernel(
    lengths, handoff, routes, q_ref, gain_ref, router_ref, kv_hbm, wg_hbm, wu_hbm, wd_hbm, out_ref,
    kv, wg, wu, wd, gathered, x, hidden, part, from_core, sum_core, from_first,
    sum_first, from_second, own_sum, sum_second, from_partner, own_rows, own_gate,
    kv_sem, w_sem, g_send, g_recv, r_send, r_recv,
):
    me = lax.axis_index("attn")
    z, y, core = me // 4, (me // 2) % 2, me % 2
    zp, zh = z % 2, z // 2
    sibling, across = me + 1 - 2 * core, me + 2 - 4 * y
    beside = me + 4 - 8 * zp
    partner = me + 8 - 16 * zh
    width = q_ref.shape[1]
    half = width // 2
    chunks = width // COLS

    def remote(src, dst, send, recv, to):
        return pltpu.make_async_remote_copy(
            src_ref=src, dst_ref=dst, send_sem=send, recv_sem=recv,
            device_id={"attn": to}, device_id_type=MESH,
        )

    barrier = pltpu.get_barrier_semaphore()

    def greet(to):
        pl.semaphore_signal(barrier, inc=1, device_id={"attn": to}, device_id_type=MESH)

    pl.when(z < 3)(lambda: greet(me + 4))
    pl.when(z > 0)(lambda: greet(me - 4))
    for to in (across, sibling, partner):
        greet(to)

    kv_copy = pltpu.make_async_copy(kv_hbm, kv, kv_sem)
    kv_copy.start()
    loads = []
    for index, (src, dst) in enumerate(((wg_hbm, wg), (wu_hbm, wu), (wd_hbm, wd))):
        size = dst.shape[0] // PIECES
        for piece in range(PIECES):
            rows = pl.ds(piece * size, size)
            loads.append(pltpu.make_async_copy(src.at[rows], dst.at[rows], w_sem.at[index, piece]))

    started = [0]

    def load(amount):
        for copy in loads[started[0]:started[0] + amount]:
            copy.start()
        started[0] += amount

    h0, h1 = handoff[0, 0], handoff[0, 1]
    low, high = jnp.minimum(h0, h1), jnp.maximum(h0, h1)

    def order_of(shape):
        row = lax.broadcasted_iota(jnp.int32, shape, 0)
        kept = row + (row >= low).astype(jnp.int32)
        kept = kept + (kept >= high).astype(jnp.int32)
        return jnp.where(row == 6, h0, jnp.where(row == 7, h1, kept))

    slot = lax.broadcasted_iota(jnp.int32, (ROWS, 128), 0)
    place = slot - (slot > h0).astype(jnp.int32) - (slot > h1).astype(jnp.int32)
    source = jnp.where(
        slot == h0, partner * ROWS + 6, jnp.where(slot == h1, partner * ROWS + 7, me * ROWS + place)
    )
    route = jnp.zeros((ROWS, 128), jnp.int32)
    for t in range(ROWS):
        route = jnp.where(slot == t, routes[t], route)
    gathered[me, :, half:] = jnp.concatenate(
        [jnp.where(route == e, source, -1).astype(F32) for e in range(EXPERTS)], axis=0
    ).astype(BF16)

    order = order_of((ROWS, ROWS))
    pick = (lax.broadcasted_iota(jnp.int32, (ROWS, ROWS), 1) == order).astype(BF16)
    queries = jnp.dot(pick, q_ref[...], preferred_element_type=F32)
    span = (ROWS, ROWS * LMAX)
    column = lax.broadcasted_iota(jnp.int32, span, 1)
    holder = jnp.zeros(span, jnp.int32)
    for t in range(1, ROWS):
        holder = holder + (column >= t * LMAX).astype(jnp.int32)
    position = column - holder * LMAX
    wide = order_of(span)
    limit = jnp.zeros(span, jnp.int32)
    for t in range(ROWS):
        limit = jnp.where(wide == t, lengths[t], limit)
    visible = jnp.where((holder == wide) & (position < limit), 0.0, -jnp.inf).astype(F32)
    visible = jnp.concatenate([visible] * GROUP, axis=0)
    kv_copy.wait()
    load(FIRST)

    def head(k):
        begin = k * GROUP * HD
        rows = jnp.concatenate(
            [queries[:, begin + g * HD:begin + (g + 1) * HD] for g in range(GROUP)], axis=0
        ).astype(BF16)
        keys = kv[:, :, k * HD:(k + 1) * HD].reshape(ROWS * LMAX, HD)
        values = kv[:, :, (KVH + k) * HD:(KVH + k + 1) * HD].reshape(ROWS * LMAX, HD)
        scores = lax.dot_general(
            rows, keys, (((1,), (1,)), ((), ())), preferred_element_type=F32
        ) * HD ** (-0.5) + visible
        weights = jnp.exp(scores - jnp.max(scores, axis=-1, keepdims=True))
        weights = (weights / jnp.sum(weights, axis=-1, keepdims=True)).astype(BF16)
        return jnp.dot(weights, values, preferred_element_type=F32)

    for k in range(KVH // 2):
        left, right = head(k), head(k + KVH // 2)
        for g in range(GROUP):
            rows = slice(g * ROWS, (g + 1) * ROWS)
            at = (k * GROUP + g) * HD
            gathered[me, :, at:at + HD] = jnp.concatenate([left[rows], right[rows]], axis=0).astype(BF16)

    pl.semaphore_wait(barrier, 3 + (z < 3).astype(jnp.int32) + (z > 0).astype(jnp.int32))

    UP, DOWN, ACROSS, CORE = range(4)

    def send(kind, block, piece, to):
        size = (half + 128) // 128 // PARTS * 128
        begin = piece * size
        size = size if piece < PARTS - 1 else half + 128 - begin
        ref = gathered.at[block, :, pl.ds(begin, size)]
        return remote(ref, ref, g_send.at[kind, block, piece], g_recv.at[block, piece], to)

    def arrived(block, piece):
        send(CORE, block, piece, sibling).wait_recv()

    def spread(finish):
        def act(copy):
            copy.wait_send() if finish else copy.start()

        def first(block, piece):
            act(send(ACROSS, block, piece, across))
            act(send(CORE, block, piece, sibling))

        for piece in range(PARTS):
            pl.when(z < 3)(lambda: act(send(UP, me, piece, me + 4)))
            pl.when(z > 0)(lambda: act(send(DOWN, me, piece, me - 4)))
            first(me, piece)

        def from_below(far, piece):
            block = me - 4 * far
            if not finish:
                arrived(block, piece)
            pl.when(z < 3)(lambda: act(send(UP, block, piece, me + 4)))
            first(block, piece)

        def from_above(far, piece):
            block = me + 4 * far
            if not finish:
                arrived(block, piece)
            pl.when(z > 0)(lambda: act(send(DOWN, block, piece, me - 4)))
            first(block, piece)

        def hand_on(block, piece):
            if not finish:
                arrived(block, piece)
            act(send(CORE, block, piece, sibling))

        for far in range(1, 4):
            for piece in range(PARTS):
                pl.when(z >= far)(functools.partial(from_below, far, piece))
                pl.when(z + far < 4)(functools.partial(from_above, far, piece))
        for piece in range(PARTS):
            hand_on(across, piece)
        for far in range(1, 4):
            for piece in range(PARTS):
                pl.when(z >= far)(functools.partial(hand_on, across - 4 * far, piece))
                pl.when(z + far < 4)(functools.partial(hand_on, across + 4 * far, piece))

    spread(False)
    def sibling_wait(chip, carry):
        for piece in range(PARTS):
            arrived(chip * 2 + 1 - core, piece)
        return carry

    lax.fori_loop(0, RANKS // 2, sibling_wait, 0)

    load(len(loads) - started[0])

    def halves(first, second):
        return (
            jnp.concatenate([first[:ROWS], second[:ROWS]], axis=0),
            jnp.concatenate([first[ROWS:], second[ROWS:]], axis=0),
        )

    def norm(left, right):
        total = jnp.sum(left * left, axis=-1, keepdims=True) + jnp.sum(
            right * right, axis=-1, keepdims=True
        )
        scale = lax.rsqrt(total / width + 1e-05)
        return (
            (left * scale * gain_ref[pl.ds(0, half)].astype(F32)[None, :]).astype(BF16),
            (right * scale * gain_ref[pl.ds(half, half)].astype(F32)[None, :]).astype(BF16),
        )

    def norm_step(chip, carry):
        left, right = halves(gathered[2 * chip, :, :half].astype(F32), gathered[2 * chip + 1, :, :half].astype(F32))
        left, right = norm(left, right)
        rows = pl.ds(pl.multiple_of(chip * 16, 16), 16)
        x[rows, :half] = left
        x[rows, half:] = right
        return carry

    lax.fori_loop(0, RANKS // 2, norm_step, 0)

    for copy in loads[:2 * PIECES]:
        copy.wait()

    def up_step(tile, carry):
        columns = pl.ds(pl.multiple_of(tile * 256, 256), 256)
        gated = jnp.dot(x[...], wg[:, columns], preferred_element_type=F32)
        upward = jnp.dot(x[...], wu[:, columns], preferred_element_type=F32)
        hidden[:, columns] = (gated / (1.0 + jnp.exp(-gated)) * upward).astype(BF16)
        return carry

    lax.fori_loop(0, wg.shape[1] // 256, up_step, 0)

    chosen = []
    for spot in range(RANKS):
        rank = (spot % 2 * 2 + spot // 2 % 2) * 4 + spot // 4 % 2 * 2 + spot // 8
        codes = gathered[rank, :, half:].astype(F32)
        chosen.append(jnp.where(zh == 0, codes[:ROWS], codes[ROWS:]))
    chosen = jnp.concatenate(chosen, axis=0)
    lane = lax.broadcasted_iota(jnp.int32, chosen.shape, 1).astype(F32)
    select = (lane == chosen).astype(BF16)
    hidden[...] = jnp.dot(select, hidden[...], preferred_element_type=F32).astype(BF16)
    for copy in loads[2 * PIECES:]:
        copy.wait()

    def core_copy(j):
        return remote(
            part.at[j, 1 - core], from_core.at[j], r_send.at[0, j], r_recv.at[0, j], sibling
        )

    def first_copy(j):
        if j % 3 != 2:
            return remote(
                sum_core.at[j, 1 - y], from_first.at[j], r_send.at[1, j], r_recv.at[1, j], across
            )
        return remote(
            sum_core.at[j, :, 1 - zp], from_first.at[j], r_send.at[1, j], r_recv.at[1, j], beside
        )

    def second_copy(j):
        if j % 3 != 2:
            return remote(
                sum_first.at[j, 1 - zp], from_second.at[j], r_send.at[2, j], r_recv.at[2, j], beside
            )
        return remote(
            sum_first.at[j, 1 - y], from_second.at[j], r_send.at[2, j], r_recv.at[2, j], across
        )

    def partner_copy(j):
        return remote(
            sum_second.at[j], from_partner.at[j], r_send.at[3, j], r_recv.at[3, j], partner
        )

    def down(j):
        part[j] = jnp.dot(
            hidden[...], wd[:, j * COLS:(j + 1) * COLS], preferred_element_type=F32
        ).astype(BF16).reshape(2, 2, 2, 16, COLS)
        core_copy(j).start()

    def add_core(j):
        core_copy(j).wait_recv()
        sum_core[j] = (part[j, core].astype(F32) + from_core[j].astype(F32)).astype(BF16)
        first_copy(j).start()

    def add_first(j):
        first_copy(j).wait_recv()
        mine = sum_core[j, y] if j % 3 != 2 else sum_core[j, :, zp]
        sum_first[j] = (mine.astype(F32) + from_first[j].astype(F32)).astype(BF16)
        second_copy(j).start()

    def add_second(j):
        second_copy(j).wait_recv()
        mine = sum_first[j, zp] if j % 3 != 2 else sum_first[j, y]
        total = mine.astype(F32) + from_second[j].astype(F32)
        upper = zh == 1
        own_sum[j] = jnp.where(upper, total[ROWS:], total[:ROWS])
        other = jnp.where(upper, total[:ROWS], total[ROWS:])
        sum_second[j] = jnp.concatenate(
            [other[:, :COLS // 2], other[:, COLS // 2:]], axis=0
        ).astype(BF16)
        partner_copy(j).start()

    def own():
        near = jnp.where(
            slot == h0, ROWS + 6, jnp.where(slot == h1, ROWS + 7, place)
        )[:, :2 * ROWS]
        take = (lax.broadcasted_iota(jnp.int32, near.shape, 1) == near).astype(BF16)
        left, right = halves(gathered[me, :, :half].astype(F32), gathered[partner, :, :half].astype(F32))
        left = jnp.dot(take, left.astype(BF16), preferred_element_type=F32)
        right = jnp.dot(take, right.astype(BF16), preferred_element_type=F32)
        own_rows[:, :half] = left
        own_rows[:, half:] = right
        left, right = norm(left, right)
        logits = []
        for e in range(EXPERTS):
            weight = router_ref[e:e + 1, :].astype(F32)
            logits.append(
                jnp.sum(left.astype(F32) * weight[:, :half], axis=-1, keepdims=True)
                + jnp.sum(right.astype(F32) * weight[:, half:], axis=-1, keepdims=True)
            )
        chosen_logit = jnp.where(route[:, :1] == 0, logits[0], logits[1])
        odds = jnp.exp(logits[0] - chosen_logit) + jnp.exp(logits[1] - chosen_logit)
        own_gate[...] = jnp.broadcast_to(1.0 / odds, own_gate.shape)

    def finish(j):
        partner_copy(j).wait_recv()
        other = from_partner[j].astype(F32)
        other = jnp.concatenate([other[:ROWS], other[ROWS:]], axis=1)
        columns = slice(j * COLS, (j + 1) * COLS)
        out_ref[:, columns] = (
            own_rows[:, columns] + own_gate[:, :1] * (own_sum[j] + other)
        ).astype(BF16)

    for step in range(chunks + LAGS[-1]):
        if step < chunks:
            down(step)
        if step == chunks - 1:
            own()
        for late, act in zip(LAGS, (add_core, add_first, add_second, finish)):
            if 0 <= step - late < chunks:
                act(step - late)

    spread(True)
    for j in range(chunks):
        for copy in (core_copy, first_copy, second_copy, partner_copy):
            copy(j).wait_send()


def fused(queries, kv_cache, lengths, handoff, routes, norm_gain, router, gate_proj, up_proj, down_proj):
    width = queries.shape[1]
    inner = gate_proj.shape[1]
    chunks = width // COLS
    smem = pl.BlockSpec(memory_space=pltpu.SMEM)
    vmem = pl.BlockSpec(memory_space=pltpu.VMEM)
    hbm = pl.BlockSpec(memory_space=pl.ANY)
    dma = pltpu.SemaphoreType.DMA
    return pl.pallas_call(
        layer_kernel,
        out_shape=jax.ShapeDtypeStruct(queries.shape, BF16),
        in_specs=[smem, smem, smem, vmem, vmem, vmem, hbm, hbm, hbm, hbm],
        out_specs=vmem,
        scratch_shapes=[
            pltpu.VMEM(kv_cache.shape, BF16),
            pltpu.VMEM(gate_proj.shape, BF16),
            pltpu.VMEM(up_proj.shape, BF16),
            pltpu.VMEM(down_proj.shape, BF16),
            pltpu.VMEM((RANKS, 2 * ROWS, width // 2 + 128), BF16),
            pltpu.VMEM((RANKS * ROWS, width), BF16),
            pltpu.VMEM((RANKS * ROWS, inner), BF16),
            pltpu.VMEM((chunks, 2, 2, 2, 16, COLS), BF16),
            pltpu.VMEM((chunks, 2, 2, 16, COLS), BF16),
            pltpu.VMEM((chunks, 2, 2, 16, COLS), BF16),
            pltpu.VMEM((chunks, 2, 16, COLS), BF16),
            pltpu.VMEM((chunks, 2, 16, COLS), BF16),
            pltpu.VMEM((chunks, 16, COLS), BF16),
            pltpu.VMEM((chunks, ROWS, COLS), F32),
            pltpu.VMEM((chunks, 16, COLS // 2), BF16),
            pltpu.VMEM((chunks, 16, COLS // 2), BF16),
            pltpu.VMEM((ROWS, width), F32),
            pltpu.VMEM((ROWS, 128), F32),
            dma,
            dma((3, PIECES)),
            dma((4, RANKS, PARTS)),
            dma((RANKS, PARTS)),
            dma((4, chunks)),
            dma((4, chunks)),
        ],
        compiler_params=pltpu.CompilerParams(
            collective_id=0, has_side_effects=True, vmem_limit_bytes=60 * 1024 * 1024
        ),
        cost_estimate=pl.CostEstimate(
            flops=6 * RANKS * ROWS * width * inner,
            bytes_accessed=6 * width * inner,
            transcendentals=0,
        ),
    )(
        lengths, handoff, routes[:, 0], queries, norm_gain, router.T, kv_cache,
        gate_proj, up_proj, down_proj,
    )


def partner(array, axis, distance):
    return lax.ppermute(array, axis, [(i, i ^ 1 << distance) for i in range(lax.axis_size(axis))])


def attend(query_rows, cache_rows, length_rows):
    total_rows = query_rows.shape[0]
    width_kv = KVH * HD
    heads_q = query_rows.reshape(total_rows, KVH, HQ // KVH, HD)
    keys_all = cache_rows[:, :, :width_kv].reshape(total_rows, LMAX, KVH, HD)
    values_all = cache_rows[:, :, width_kv:].reshape(total_rows, LMAX, KVH, HD)
    scores = jnp.einsum(
        "rkgd,rtkd->rkgt", heads_q, keys_all, preferred_element_type=jnp.float32
    ) * HD ** (-0.5)
    visible = jnp.arange(LMAX, dtype=jnp.int32)[None, :] < length_rows[:, None]
    scores = jnp.where(visible[:, None, None, :], scores, -jnp.inf)
    highest = jnp.max(scores, axis=-1, keepdims=True)
    weights = jnp.exp(scores - highest)
    weights = (weights / jnp.sum(weights, axis=-1, keepdims=True)).astype(jnp.bfloat16)
    mixed_heads = jnp.einsum(
        "rkgt,rtkd->rkgd", weights, values_all, preferred_element_type=jnp.float32
    )
    return mixed_heads.reshape(total_rows, HQ * HD).astype(jnp.bfloat16)


def body(
    queries, kv_cache, lengths, handoff, routes, norm_gain, router, gate_proj, up_proj, down_proj
):
    ranks = lax.axis_size("attn")
    if ranks == RANKS and queries.shape[0] == ROWS:
        return fused(
            queries, kv_cache, lengths, handoff, routes, norm_gain, router,
            gate_proj, up_proj, down_proj,
        )
    picks = handoff[0]
    highest_bit = ranks.bit_length() - 2
    attended = attend(queries, kv_cache, lengths)
    attended = attended.at[picks].set(partner(attended[picks], "attn", highest_bit))
    attended_f = attended.astype(jnp.float32)
    scale_rows = lax.rsqrt(jnp.mean(attended_f * attended_f, axis=-1, keepdims=True) + 1e-05)
    normed = (attended_f * scale_rows * norm_gain.astype(jnp.float32)).astype(jnp.bfloat16)
    logits = jnp.dot(normed, router, preferred_element_type=jnp.float32)
    chosen_logit = jnp.take_along_axis(logits, routes, axis=1)
    gate_prob = 1.0 / jnp.sum(jnp.exp(logits - chosen_logit), axis=1)
    chosen_expert = routes[:, 0]
    row_order = jnp.arange(chosen_expert.shape[0], dtype=jnp.int32)
    earlier = (chosen_expert[:, None] == chosen_expert[None, :]) & (
        row_order[None, :] < row_order[:, None]
    )
    slot_index = jnp.sum(earlier.astype(jnp.int32), axis=1)
    target = chosen_expert * CAP + slot_index
    selector = (jnp.arange(EXPERTS * CAP, dtype=jnp.int32)[:, None] == target[None, :]).astype(
        jnp.bfloat16
    )
    width = normed.shape[1]
    dispatch = (
        jnp.dot(selector, normed, preferred_element_type=jnp.float32)
        .astype(jnp.bfloat16)
        .reshape(EXPERTS, CAP, width)
    )
    group_size = ranks // EXPERTS
    mine = lax.axis_index("attn") // group_size
    own_rows = lax.dynamic_index_in_dim(
        lax.all_gather(dispatch[None], "attn", axis=0, tiled=True), mine, 1, keepdims=False
    )
    flat = own_rows.reshape(-1, width)
    gated = jnp.dot(flat, gate_proj, preferred_element_type=jnp.float32)
    upward = jnp.dot(flat, up_proj, preferred_element_type=jnp.float32)
    hidden = (jax.nn.silu(gated) * upward).astype(jnp.bfloat16)
    partial_out = jnp.dot(hidden, down_proj, preferred_element_type=jnp.float32).astype(
        jnp.bfloat16
    )
    partials = partial_out.reshape(own_rows.shape)
    received = lax.all_to_all(partials, "attn", split_axis=0, concat_axis=0, tiled=True)
    summed = received.astype(jnp.float32).reshape(EXPERTS, group_size, CAP, width).sum(axis=1)
    expert_value = jnp.take(summed.reshape(EXPERTS * CAP, width), target, axis=0)
    return (attended_f + gate_prob[:, None] * expert_value).astype(jnp.bfloat16)


def solution(mesh):
    return jax.shard_map(
        body,
        mesh=mesh,
        in_specs=(
            P(("groups", "attn"), None),
            P(("groups", "attn"), None, None),
            P(("groups", "attn")),
            P(("groups", "attn"), None),
            P(("groups", "attn"), None),
            P(),
            P(),
            P(None, "attn"),
            P(None, "attn"),
            P("attn", None),
        ),
        out_specs=P(("groups", "attn"), None),
        check_vma=False,
    )
```

```python
import functools
import jax
import jax.numpy as jnp
from jax import lax
from jax.experimental import pallas as pl
from jax.experimental.pallas import tpu as pltpu
from jax.sharding import PartitionSpec as P

HQ = 48
KVH = 8
HD = 128
EXPERTS = 2
LMAX = 48
CAP = 6
GROUP = HQ // KVH
MESH = pl.DeviceIdType.MESH
F32 = jnp.float32
BF16 = jnp.bfloat16
RANKS = 16
ROWS = 8
PIECES = 8
FIRST = 24
PARTS = 2
LAGS = (2, 5, 8, 11)
COLS = 1024


def layer_kernel(
    lengths, handoff, routes, q_ref, gain_ref, router_ref, kv_hbm, wg_hbm, wu_hbm, wd_hbm, out_ref,
    kv, wg, wu, wd, gathered, x, hidden, part, from_core, sum_core, from_first,
    sum_first, from_second, own_sum, sum_second, from_partner, own_rows, own_gate,
    kv_sem, w_sem, g_send, g_recv, r_send, r_recv,
):
    me = lax.axis_index("attn")
    z, y, core = me // 4, (me // 2) % 2, me % 2
    zp, zh = z % 2, z // 2
    sibling, across = me + 1 - 2 * core, me + 2 - 4 * y
    beside = me + 4 - 8 * zp
    partner = me + 8 - 16 * zh
    width = q_ref.shape[1]
    half = width // 2
    chunks = width // COLS

    def remote(src, dst, send, recv, to):
        return pltpu.make_async_remote_copy(
            src_ref=src, dst_ref=dst, send_sem=send, recv_sem=recv,
            device_id={"attn": to}, device_id_type=MESH,
        )

    barrier = pltpu.get_barrier_semaphore()

    def greet(to):
        pl.semaphore_signal(barrier, inc=1, device_id={"attn": to}, device_id_type=MESH)

    pl.when(z < 3)(lambda: greet(me + 4))
    pl.when(z > 0)(lambda: greet(me - 4))
    for to in (across, sibling, partner):
        greet(to)

    kv_copy = pltpu.make_async_copy(kv_hbm, kv, kv_sem)
    kv_copy.start()
    loads = []
    for index, (src, dst) in enumerate(((wg_hbm, wg), (wu_hbm, wu), (wd_hbm, wd))):
        size = dst.shape[0] // PIECES
        for piece in range(PIECES):
            rows = pl.ds(piece * size, size)
            loads.append(pltpu.make_async_copy(src.at[rows], dst.at[rows], w_sem.at[index, piece]))

    started = [0]

    def load(amount):
        for copy in loads[started[0]:started[0] + amount]:
            copy.start()
        started[0] += amount

    h0, h1 = handoff[0, 0], handoff[0, 1]
    low, high = jnp.minimum(h0, h1), jnp.maximum(h0, h1)

    def order_of(shape):
        row = lax.broadcasted_iota(jnp.int32, shape, 0)
        kept = row + (row >= low).astype(jnp.int32)
        kept = kept + (kept >= high).astype(jnp.int32)
        return jnp.where(row == 6, h0, jnp.where(row == 7, h1, kept))

    slot = lax.broadcasted_iota(jnp.int32, (ROWS, 128), 0)
    place = slot - (slot > h0).astype(jnp.int32) - (slot > h1).astype(jnp.int32)
    source = jnp.where(
        slot == h0, partner * ROWS + 6, jnp.where(slot == h1, partner * ROWS + 7, me * ROWS + place)
    )
    route = jnp.zeros((ROWS, 128), jnp.int32)
    for t in range(ROWS):
        route = jnp.where(slot == t, routes[t], route)
    gathered[me, :, half:] = jnp.concatenate(
        [jnp.where(route == e, source, -1).astype(F32) for e in range(EXPERTS)], axis=0
    ).astype(BF16)

    order = order_of((ROWS, ROWS))
    pick = (lax.broadcasted_iota(jnp.int32, (ROWS, ROWS), 1) == order).astype(BF16)
    queries = jnp.dot(pick, q_ref[...], preferred_element_type=F32)
    span = (ROWS, ROWS * LMAX)
    column = lax.broadcasted_iota(jnp.int32, span, 1)
    holder = jnp.zeros(span, jnp.int32)
    for t in range(1, ROWS):
        holder = holder + (column >= t * LMAX).astype(jnp.int32)
    position = column - holder * LMAX
    wide = order_of(span)
    limit = jnp.zeros(span, jnp.int32)
    for t in range(ROWS):
        limit = jnp.where(wide == t, lengths[t], limit)
    visible = jnp.where((holder == wide) & (position < limit), 0.0, -jnp.inf).astype(F32)
    visible = jnp.concatenate([visible] * GROUP, axis=0)
    kv_copy.wait()
    load(FIRST)

    def head(k):
        begin = k * GROUP * HD
        rows = jnp.concatenate(
            [queries[:, begin + g * HD:begin + (g + 1) * HD] for g in range(GROUP)], axis=0
        ).astype(BF16)
        keys = kv[:, :, k * HD:(k + 1) * HD].reshape(ROWS * LMAX, HD)
        values = kv[:, :, (KVH + k) * HD:(KVH + k + 1) * HD].reshape(ROWS * LMAX, HD)
        scores = lax.dot_general(
            rows, keys, (((1,), (1,)), ((), ())), preferred_element_type=F32
        ) * HD ** (-0.5) + visible
        weights = jnp.exp(scores - jnp.max(scores, axis=-1, keepdims=True))
        weights = (weights / jnp.sum(weights, axis=-1, keepdims=True)).astype(BF16)
        return jnp.dot(weights, values, preferred_element_type=F32)

    for k in range(KVH // 2):
        left, right = head(k), head(k + KVH // 2)
        for g in range(GROUP):
            rows = slice(g * ROWS, (g + 1) * ROWS)
            at = (k * GROUP + g) * HD
            gathered[me, :, at:at + HD] = jnp.concatenate([left[rows], right[rows]], axis=0).astype(BF16)

    pl.semaphore_wait(barrier, 3 + (z < 3).astype(jnp.int32) + (z > 0).astype(jnp.int32))

    UP, DOWN, ACROSS, CORE = range(4)

    def send(kind, block, piece, to):
        size = (half + 128) // 128 // PARTS * 128
        begin = piece * size
        size = size if piece < PARTS - 1 else half + 128 - begin
        ref = gathered.at[block, :, pl.ds(begin, size)]
        return remote(ref, ref, g_send.at[kind, block, piece], g_recv.at[block, piece], to)

    def arrived(block, piece):
        send(CORE, block, piece, sibling).wait_recv()

    def spread(finish):
        def act(copy):
            copy.wait_send() if finish else copy.start()

        def first(block, piece):
            act(send(ACROSS, block, piece, across))
            act(send(CORE, block, piece, sibling))

        for piece in range(PARTS):
            pl.when(z < 3)(lambda: act(send(UP, me, piece, me + 4)))
            pl.when(z > 0)(lambda: act(send(DOWN, me, piece, me - 4)))
            first(me, piece)

        def from_below(far, piece):
            block = me - 4 * far
            if not finish:
                arrived(block, piece)
            pl.when(z < 3)(lambda: act(send(UP, block, piece, me + 4)))
            first(block, piece)

        def from_above(far, piece):
            block = me + 4 * far
            if not finish:
                arrived(block, piece)
            pl.when(z > 0)(lambda: act(send(DOWN, block, piece, me - 4)))
            first(block, piece)

        def hand_on(block, piece):
            if not finish:
                arrived(block, piece)
            act(send(CORE, block, piece, sibling))

        for far in range(1, 4):
            for piece in range(PARTS):
                pl.when(z >= far)(functools.partial(from_below, far, piece))
                pl.when(z + far < 4)(functools.partial(from_above, far, piece))
        for piece in range(PARTS):
            hand_on(across, piece)
        for far in range(1, 4):
            for piece in range(PARTS):
                pl.when(z >= far)(functools.partial(hand_on, across - 4 * far, piece))
                pl.when(z + far < 4)(functools.partial(hand_on, across + 4 * far, piece))

    spread(False)
    def sibling_wait(chip, carry):
        for piece in range(PARTS):
            arrived(chip * 2 + 1 - core, piece)
        return carry

    lax.fori_loop(0, RANKS // 2, sibling_wait, 0)

    load(len(loads) - started[0])

    def halves(first, second):
        return (
            jnp.concatenate([first[:ROWS], second[:ROWS]], axis=0),
            jnp.concatenate([first[ROWS:], second[ROWS:]], axis=0),
        )

    def norm(left, right):
        total = jnp.sum(left * left, axis=-1, keepdims=True) + jnp.sum(
            right * right, axis=-1, keepdims=True
        )
        scale = lax.rsqrt(total / width + 1e-05)
        return (
            (left * scale * gain_ref[pl.ds(0, half)].astype(F32)[None, :]).astype(BF16),
            (right * scale * gain_ref[pl.ds(half, half)].astype(F32)[None, :]).astype(BF16),
        )

    def norm_step(chip, carry):
        left, right = halves(gathered[2 * chip, :, :half].astype(F32), gathered[2 * chip + 1, :, :half].astype(F32))
        left, right = norm(left, right)
        rows = pl.ds(pl.multiple_of(chip * 16, 16), 16)
        x[rows, :half] = left
        x[rows, half:] = right
        return carry

    lax.fori_loop(0, RANKS // 2, norm_step, 0)

    for copy in loads[:2 * PIECES]:
        copy.wait()

    def up_step(tile, carry):
        columns = pl.ds(pl.multiple_of(tile * 256, 256), 256)
        gated = jnp.dot(x[...], wg[:, columns], preferred_element_type=F32)
        upward = jnp.dot(x[...], wu[:, columns], preferred_element_type=F32)
        hidden[:, columns] = (gated / (1.0 + jnp.exp(-gated)) * upward).astype(BF16)
        return carry

    lax.fori_loop(0, wg.shape[1] // 256, up_step, 0)

    chosen = []
    for spot in range(RANKS):
        rank = (spot % 2 * 2 + spot // 2 % 2) * 4 + spot // 4 % 2 * 2 + spot // 8
        codes = gathered[rank, :, half:].astype(F32)
        chosen.append(jnp.where(zh == 0, codes[:ROWS], codes[ROWS:]))
    chosen = jnp.concatenate(chosen, axis=0)
    lane = lax.broadcasted_iota(jnp.int32, chosen.shape, 1).astype(F32)
    select = (lane == chosen).astype(BF16)
    hidden[...] = jnp.dot(select, hidden[...], preferred_element_type=F32).astype(BF16)
    for copy in loads[2 * PIECES:]:
        copy.wait()

    def core_copy(j):
        return remote(
            part.at[j, 1 - core], from_core.at[j], r_send.at[0, j], r_recv.at[0, j], sibling
        )

    def first_copy(j):
        if j % 3 != 1:
            return remote(
                sum_core.at[j, 1 - y], from_first.at[j], r_send.at[1, j], r_recv.at[1, j], across
            )
        return remote(
            sum_core.at[j, :, 1 - zp], from_first.at[j], r_send.at[1, j], r_recv.at[1, j], beside
        )

    def second_copy(j):
        if j % 3 != 1:
            return remote(
                sum_first.at[j, 1 - zp], from_second.at[j], r_send.at[2, j], r_recv.at[2, j], beside
            )
        return remote(
            sum_first.at[j, 1 - y], from_second.at[j], r_send.at[2, j], r_recv.at[2, j], across
        )

    def partner_copy(j):
        return remote(
            sum_second.at[j], from_partner.at[j], r_send.at[3, j], r_recv.at[3, j], partner
        )

    def down(j):
        part[j] = jnp.dot(
            hidden[...], wd[:, j * COLS:(j + 1) * COLS], preferred_element_type=F32
        ).astype(BF16).reshape(2, 2, 2, 16, COLS)
        core_copy(j).start()

    def add_core(j):
        core_copy(j).wait_recv()
        sum_core[j] = (part[j, core].astype(F32) + from_core[j].astype(F32)).astype(BF16)
        first_copy(j).start()

    def add_first(j):
        first_copy(j).wait_recv()
        mine = sum_core[j, y] if j % 3 != 1 else sum_core[j, :, zp]
        sum_first[j] = (mine.astype(F32) + from_first[j].astype(F32)).astype(BF16)
        second_copy(j).start()

    def add_second(j):
        second_copy(j).wait_recv()
        mine = sum_first[j, zp] if j % 3 != 1 else sum_first[j, y]
        total = mine.astype(F32) + from_second[j].astype(F32)
        upper = zh == 1
        own_sum[j] = jnp.where(upper, total[ROWS:], total[:ROWS])
        other = jnp.where(upper, total[:ROWS], total[ROWS:])
        sum_second[j] = jnp.concatenate(
            [other[:, :COLS // 2], other[:, COLS // 2:]], axis=0
        ).astype(BF16)
        partner_copy(j).start()

    def own():
        near = jnp.where(
            slot == h0, ROWS + 6, jnp.where(slot == h1, ROWS + 7, place)
        )[:, :2 * ROWS]
        take = (lax.broadcasted_iota(jnp.int32, near.shape, 1) == near).astype(BF16)
        left, right = halves(gathered[me, :, :half].astype(F32), gathered[partner, :, :half].astype(F32))
        left = jnp.dot(take, left.astype(BF16), preferred_element_type=F32)
        right = jnp.dot(take, right.astype(BF16), preferred_element_type=F32)
        own_rows[:, :half] = left
        own_rows[:, half:] = right
        left, right = norm(left, right)
        logits = []
        for e in range(EXPERTS):
            weight = router_ref[e:e + 1, :].astype(F32)
            logits.append(
                jnp.sum(left.astype(F32) * weight[:, :half], axis=-1, keepdims=True)
                + jnp.sum(right.astype(F32) * weight[:, half:], axis=-1, keepdims=True)
            )
        chosen_logit = jnp.where(route[:, :1] == 0, logits[0], logits[1])
        odds = jnp.exp(logits[0] - chosen_logit) + jnp.exp(logits[1] - chosen_logit)
        own_gate[...] = jnp.broadcast_to(1.0 / odds, own_gate.shape)

    def finish(j):
        partner_copy(j).wait_recv()
        other = from_partner[j].astype(F32)
        other = jnp.concatenate([other[:ROWS], other[ROWS:]], axis=1)
        columns = slice(j * COLS, (j + 1) * COLS)
        out_ref[:, columns] = (
            own_rows[:, columns] + own_gate[:, :1] * (own_sum[j] + other)
        ).astype(BF16)

    for step in range(chunks + LAGS[-1]):
        if step < chunks:
            down(step)
        if step == chunks - 1:
            own()
        for late, act in zip(LAGS, (add_core, add_first, add_second, finish)):
            if 0 <= step - late < chunks:
                act(step - late)

    spread(True)
    for j in range(chunks):
        for copy in (core_copy, first_copy, second_copy, partner_copy):
            copy(j).wait_send()


def fused(queries, kv_cache, lengths, handoff, routes, norm_gain, router, gate_proj, up_proj, down_proj):
    width = queries.shape[1]
    inner = gate_proj.shape[1]
    chunks = width // COLS
    smem = pl.BlockSpec(memory_space=pltpu.SMEM)
    vmem = pl.BlockSpec(memory_space=pltpu.VMEM)
    hbm = pl.BlockSpec(memory_space=pl.ANY)
    dma = pltpu.SemaphoreType.DMA
    return pl.pallas_call(
        layer_kernel,
        out_shape=jax.ShapeDtypeStruct(queries.shape, BF16),
        in_specs=[smem, smem, smem, vmem, vmem, vmem, hbm, hbm, hbm, hbm],
        out_specs=vmem,
        scratch_shapes=[
            pltpu.VMEM(kv_cache.shape, BF16),
            pltpu.VMEM(gate_proj.shape, BF16),
            pltpu.VMEM(up_proj.shape, BF16),
            pltpu.VMEM(down_proj.shape, BF16),
            pltpu.VMEM((RANKS, 2 * ROWS, width // 2 + 128), BF16),
            pltpu.VMEM((RANKS * ROWS, width), BF16),
            pltpu.VMEM((RANKS * ROWS, inner), BF16),
            pltpu.VMEM((chunks, 2, 2, 2, 16, COLS), BF16),
            pltpu.VMEM((chunks, 2, 2, 16, COLS), BF16),
            pltpu.VMEM((chunks, 2, 2, 16, COLS), BF16),
            pltpu.VMEM((chunks, 2, 16, COLS), BF16),
            pltpu.VMEM((chunks, 2, 16, COLS), BF16),
            pltpu.VMEM((chunks, 16, COLS), BF16),
            pltpu.VMEM((chunks, ROWS, COLS), F32),
            pltpu.VMEM((chunks, 16, COLS // 2), BF16),
            pltpu.VMEM((chunks, 16, COLS // 2), BF16),
            pltpu.VMEM((ROWS, width), F32),
            pltpu.VMEM((ROWS, 128), F32),
            dma,
            dma((3, PIECES)),
            dma((4, RANKS, PARTS)),
            dma((RANKS, PARTS)),
            dma((4, chunks)),
            dma((4, chunks)),
        ],
        compiler_params=pltpu.CompilerParams(
            collective_id=0, has_side_effects=True, vmem_limit_bytes=60 * 1024 * 1024
        ),
        cost_estimate=pl.CostEstimate(
            flops=6 * RANKS * ROWS * width * inner,
            bytes_accessed=6 * width * inner,
            transcendentals=0,
        ),
    )(
        lengths, handoff, routes[:, 0], queries, norm_gain, router.T, kv_cache,
        gate_proj, up_proj, down_proj,
    )


def partner(array, axis, distance):
    return lax.ppermute(array, axis, [(i, i ^ 1 << distance) for i in range(lax.axis_size(axis))])


def attend(query_rows, cache_rows, length_rows):
    total_rows = query_rows.shape[0]
    width_kv = KVH * HD
    heads_q = query_rows.reshape(total_rows, KVH, HQ // KVH, HD)
    keys_all = cache_rows[:, :, :width_kv].reshape(total_rows, LMAX, KVH, HD)
    values_all = cache_rows[:, :, width_kv:].reshape(total_rows, LMAX, KVH, HD)
    scores = jnp.einsum(
        "rkgd,rtkd->rkgt", heads_q, keys_all, preferred_element_type=jnp.float32
    ) * HD ** (-0.5)
    visible = jnp.arange(LMAX, dtype=jnp.int32)[None, :] < length_rows[:, None]
    scores = jnp.where(visible[:, None, None, :], scores, -jnp.inf)
    highest = jnp.max(scores, axis=-1, keepdims=True)
    weights = jnp.exp(scores - highest)
    weights = (weights / jnp.sum(weights, axis=-1, keepdims=True)).astype(jnp.bfloat16)
    mixed_heads = jnp.einsum(
        "rkgt,rtkd->rkgd", weights, values_all, preferred_element_type=jnp.float32
    )
    return mixed_heads.reshape(total_rows, HQ * HD).astype(jnp.bfloat16)


def body(
    queries, kv_cache, lengths, handoff, routes, norm_gain, router, gate_proj, up_proj, down_proj
):
    ranks = lax.axis_size("attn")
    if ranks == RANKS and queries.shape[0] == ROWS:
        return fused(
            queries, kv_cache, lengths, handoff, routes, norm_gain, router,
            gate_proj, up_proj, down_proj,
        )
    picks = handoff[0]
    highest_bit = ranks.bit_length() - 2
    attended = attend(queries, kv_cache, lengths)
    attended = attended.at[picks].set(partner(attended[picks], "attn", highest_bit))
    attended_f = attended.astype(jnp.float32)
    scale_rows = lax.rsqrt(jnp.mean(attended_f * attended_f, axis=-1, keepdims=True) + 1e-05)
    normed = (attended_f * scale_rows * norm_gain.astype(jnp.float32)).astype(jnp.bfloat16)
    logits = jnp.dot(normed, router, preferred_element_type=jnp.float32)
    chosen_logit = jnp.take_along_axis(logits, routes, axis=1)
    gate_prob = 1.0 / jnp.sum(jnp.exp(logits - chosen_logit), axis=1)
    chosen_expert = routes[:, 0]
    row_order = jnp.arange(chosen_expert.shape[0], dtype=jnp.int32)
    earlier = (chosen_expert[:, None] == chosen_expert[None, :]) & (
        row_order[None, :] < row_order[:, None]
    )
    slot_index = jnp.sum(earlier.astype(jnp.int32), axis=1)
    target = chosen_expert * CAP + slot_index
    selector = (jnp.arange(EXPERTS * CAP, dtype=jnp.int32)[:, None] == target[None, :]).astype(
        jnp.bfloat16
    )
    width = normed.shape[1]
    dispatch = (
        jnp.dot(selector, normed, preferred_element_type=jnp.float32)
        .astype(jnp.bfloat16)
        .reshape(EXPERTS, CAP, width)
    )
    group_size = ranks // EXPERTS
    mine = lax.axis_index("attn") // group_size
    own_rows = lax.dynamic_index_in_dim(
        lax.all_gather(dispatch[None], "attn", axis=0, tiled=True), mine, 1, keepdims=False
    )
    flat = own_rows.reshape(-1, width)
    gated = jnp.dot(flat, gate_proj, preferred_element_type=jnp.float32)
    upward = jnp.dot(flat, up_proj, preferred_element_type=jnp.float32)
    hidden = (jax.nn.silu(gated) * upward).astype(jnp.bfloat16)
    partial_out = jnp.dot(hidden, down_proj, preferred_element_type=jnp.float32).astype(
        jnp.bfloat16
    )
    partials = partial_out.reshape(own_rows.shape)
    received = lax.all_to_all(partials, "attn", split_axis=0, concat_axis=0, tiled=True)
    summed = received.astype(jnp.float32).reshape(EXPERTS, group_size, CAP, width).sum(axis=1)
    expert_value = jnp.take(summed.reshape(EXPERTS * CAP, width), target, axis=0)
    return (attended_f + gate_prob[:, None] * expert_value).astype(jnp.bfloat16)


def solution(mesh):
    return jax.shard_map(
        body,
        mesh=mesh,
        in_specs=(
            P(("groups", "attn"), None),
            P(("groups", "attn"), None, None),
            P(("groups", "attn")),
            P(("groups", "attn"), None),
            P(("groups", "attn"), None),
            P(),
            P(),
            P(None, "attn"),
            P(None, "attn"),
            P("attn", None),
        ),
        out_specs=P(("groups", "attn"), None),
        check_vma=False,
    )
```
